128 devices in a mesh: seq: 8 (over x, core), exp: 16 (over y, z).
Axes of the slice: x: 4, y: 4, z: 4, core: 2. Of those that a mesh axis runs over, the one named last changes fastest.
Arguments:
- query_rows: bfloat16 [16, 1536, 4096], P('exp', 'seq'), may hold values from -6 to 6
- key_rows: bfloat16 [16, 1536, 512], P('exp', 'seq'), may hold values from -6 to 6
- value_matrix: bfloat16 [16, 1536, 512], P('exp', 'seq'), may hold values from -6 to 6
- doc_ids: int32 [16, 1536], P('exp'), may hold values from 0 to 7, as said below
- out_weight: bfloat16 [4096, 2048], P(('seq', 'exp')), may hold values from -0.375 to 0.375
- enc_weight: bfloat16 [128, 2048, 1024], P(('seq', 'exp')), may hold values from -0.125 to 0.125
- enc_bias: float32 [128, 1024], P(('seq', 'exp')), may hold values from -3 to 3
- dec_weight: bfloat16 [128, 1024, 2048], P(('seq', 'exp')), may hold values from -0.1875 to 0.1875
- dec_bias: float32 [2048], replicated, may hold values from -3 to 3
- expert_ids: int32 [16, 1536], P('exp', 'seq'), may hold values from 0 to 127
- slot_ids: int32 [16, 1536], P('exp', 'seq'), may hold values from -1 to 2, as said below
Outputs:
- harvested: bfloat16 [16, 1536, 2048], P('exp', 'seq')
- reconstruction: bfloat16 [16, 1536, 2048], P('exp', 'seq')
- error_rows: bfloat16 [16, 1536, 2048], P('exp', 'seq')
- dec_grad: bfloat16 [128, 1024, 2048], P(('seq', 'exp'))
The draws below stay inside these ranges and needn't reach their ends.
Inputs may be any that keep to these rules, and one draw needn't show every extreme that they name: `doc_ids`: each sequence's numbers start at 0, never fall, and rise by one at each of 7 document starts. `slot_ids`: among one device's tokens, those that name the same expert and are kept hold the slots 0 to n - 1 in some order, n at most 3; -1 marks a token left out. In every draw some expert holds all 3 slots on every device.
All inputs are finite; a program needn't handle non-finite values.
Results may differ from the reference program's by a relative error of at most 0.014.
Values may be sent and summed in bfloat16 or wider, within the bound.
A program may use at most 128 MiB of HBM per device.

```python
import math
import jax
import jax.numpy as jnp
from jax import lax

D = 2048
QUERY_HEADS = 32
KEY_VALUE_HEADS = 4
HEAD_DIMENSION = 128
F = 1024
DOCS = 8
TOK_DEV = 192
SEQUENCE_LENGTH = 1536
SEQUENCE_COUNT = 16
EXPERTS = 128
CAP = 3


def segment_table(key):
    sequence_keys = jax.random.split(key, SEQUENCE_COUNT)

    def one_sequence(sequence_key):
        cut_points = jax.random.permutation(sequence_key, SEQUENCE_LENGTH - 1)[:DOCS - 1] + 1
        places = jnp.arange(SEQUENCE_LENGTH)
        return jnp.sum(places[:, None] >= cut_points[None, :], axis=1).astype(jnp.int32)
    return jax.vmap(one_sequence)(sequence_keys)


def draw_query_rows(key, part):
    full_dimensions = (SEQUENCE_COUNT, SEQUENCE_LENGTH, QUERY_HEADS * HEAD_DIMENSION)
    value_output = jnp.clip(jax.random.normal(jax.random.fold_in(key, 41), full_dimensions), -6.0, 6.0)
    return value_output.astype(jnp.bfloat16)


def draw_key_rows(key, part):
    full_dimensions = (SEQUENCE_COUNT, SEQUENCE_LENGTH, KEY_VALUE_HEADS * HEAD_DIMENSION)
    value_output = jnp.clip(jax.random.normal(jax.random.fold_in(key, 43), full_dimensions), -6.0, 6.0)
    return value_output.astype(jnp.bfloat16)


def draw_doc_ids(key, part):
    return segment_table(jax.random.fold_in(key, 11))


def routing_tables(key):
    blocks = SEQUENCE_COUNT * (SEQUENCE_LENGTH // TOK_DEV)
    hot_count = CAP + max(1, CAP // 3)
    hot_expert = jax.random.randint(jax.random.fold_in(key, 1), (), 0, EXPERTS)
    relabel = jax.random.permutation(jax.random.fold_in(key, 2), EXPERTS - 1)
    first_pick = jax.random.randint(jax.random.fold_in(key, 3), (blocks, TOK_DEV), 0, EXPERTS - 1)
    second_pick = jax.random.randint(jax.random.fold_in(key, 4), (blocks, TOK_DEV), 0, EXPERTS - 1)
    others = (hot_expert + 1 + relabel[jnp.minimum(first_pick, second_pick)]) % EXPERTS
    order_keys = jax.random.split(jax.random.fold_in(key, 5), blocks)
    hot_rank = jax.vmap(lambda one_key: jax.random.permutation(one_key, TOK_DEV))(order_keys)
    chosen_expert = jnp.where(hot_rank < hot_count, hot_expert, others).astype(jnp.int32)
    slot_keys = jax.random.split(jax.random.fold_in(key, 6), blocks)
    priority = jax.vmap(lambda one_key: jax.random.permutation(one_key, TOK_DEV))(slot_keys)
    same_expert = chosen_expert[:, :, None] == chosen_expert[:, None, :]
    earlier = priority[:, None, :] < priority[:, :, None]
    ranking = jnp.sum(same_expert & earlier, axis=2)
    slot_table = jnp.where(ranking < CAP, ranking, -1).astype(jnp.int32)
    return (chosen_expert.reshape(SEQUENCE_COUNT, SEQUENCE_LENGTH), slot_table.reshape(SEQUENCE_COUNT, SEQUENCE_LENGTH))


def draw_expert_ids(key, part):
    return routing_tables(jax.random.fold_in(key, 23))[0]


def draw_slot_ids(key, part):
    return routing_tables(jax.random.fold_in(key, 23))[1]


def shard_levels(own_key, dims, pieces, smallest, largest):
    gain, own = 1.0, jax.random.fold_in(own_key, 6)
    for dim, shards_of in pieces:
        heights = jnp.exp(jax.random.uniform(jax.random.fold_in(own, dim), (shards_of,), jnp.float32, smallest / len(pieces), largest / len(pieces)))
        gain = gain * jnp.repeat(heights, dims[dim] // shards_of).reshape([-1 if axis == dim else 1 for axis in range(len(dims))])
    return gain


def normal_values(stream_key, extent, scale, bound, cuts=(), kind=jnp.bfloat16):
    values = jax.random.normal(stream_key, extent, jnp.float32) * scale
    if len(cuts) > 0:
        values = shard_levels(stream_key, extent, cuts, -0.22, 0.18) * values
    return jnp.clip(values, min=-bound, max=bound).astype(kind)


def setup_inputs(seed: int = 0) -> dict:
    splits = jax.random.split(jax.random.key(seed), 12)
    return {
        "query_rows": draw_query_rows(jax.random.fold_in(splits[11], 71), 0),
        "key_rows": draw_key_rows(jax.random.fold_in(splits[11], 71), 0),
        "value_matrix": normal_values(splits[2], (SEQUENCE_COUNT, SEQUENCE_LENGTH, KEY_VALUE_HEADS * HEAD_DIMENSION), 1.0, 6.0, ((0, 16), (1, 8))),
        "doc_ids": draw_doc_ids(jax.random.fold_in(splits[11], 71), 0),
        "out_weight": normal_values(splits[4], (QUERY_HEADS * HEAD_DIMENSION, D), (QUERY_HEADS * HEAD_DIMENSION // 16) ** -0.5, 0.375, ((0, 128),)),
        "enc_weight": normal_values(splits[5], (EXPERTS, D, F), D ** -0.5, 0.125, ((0, 128),)),
        "enc_bias": normal_values(splits[6], (EXPERTS, F), 0.5, 3.0, ((0, 128),), jnp.float32),
        "dec_weight": normal_values(splits[7], (EXPERTS, F, D), F ** -0.5, 0.1875, ((0, 128),)),
        "dec_bias": normal_values(splits[8], (D,), 0.5, 3.0, (), jnp.float32),
        "expert_ids": draw_expert_ids(jax.random.fold_in(splits[11], 71), 0),
        "slot_ids": draw_slot_ids(jax.random.fold_in(splits[11], 71), 0),
    }


masked_score = -1e+30

def attend_sequence(query_seq, key_sequence, value_sequence, doc_seq):
    span_length = query_seq.shape[0]
    query_group_width = QUERY_HEADS // KEY_VALUE_HEADS
    query_heads = query_seq.reshape(span_length, QUERY_HEADS, HEAD_DIMENSION).transpose(1, 0, 2)
    key_head_rows = key_sequence.reshape(span_length, KEY_VALUE_HEADS, HEAD_DIMENSION).transpose(1, 0, 2)
    value_head_rows = value_sequence.reshape(span_length, KEY_VALUE_HEADS, HEAD_DIMENSION).transpose(1, 0, 2)
    positions = jnp.arange(span_length, dtype=jnp.int32)
    visible = (positions[:, None] >= positions[None, :]) & (doc_seq[:, None] == doc_seq[None, :])
    score_scale = 1.0 / math.sqrt(HEAD_DIMENSION)

    def one_head(head_index):
        query_one = query_heads[head_index]
        key_one = key_head_rows[head_index // query_group_width]
        value_one = value_head_rows[head_index // query_group_width]
        scores = jnp.dot(query_one, key_one.T, preferred_element_type=jnp.float32) * score_scale
        scores = jnp.where(visible, scores, masked_score)
        highest = lax.optimization_barrier(jnp.max(scores, axis=1, keepdims=True))
        weights = jnp.exp(scores - highest)
        normed = (weights / lax.optimization_barrier(jnp.sum(weights, axis=1, keepdims=True))).astype(jnp.bfloat16)
        return jnp.dot(normed, value_one, preferred_element_type=jnp.float32).astype(jnp.bfloat16)
    mixed = lax.map(one_head, jnp.arange(QUERY_HEADS, dtype=jnp.int32))
    return mixed.transpose(1, 0, 2).reshape(span_length, QUERY_HEADS * HEAD_DIMENSION)

def reference(query_rows, key_rows, value_matrix, doc_ids, out_weight, enc_weight, enc_bias, dec_weight, dec_bias, expert_ids, slot_ids):

    def one_sequence(items):
        query_seq, key_sequence, value_sequence, doc_seq = items
        attended = attend_sequence(query_seq, key_sequence, value_sequence, doc_seq)
        return jnp.dot(attended, out_weight, preferred_element_type=jnp.float32).astype(jnp.bfloat16)
    harvested = lax.map(one_sequence, (query_rows, key_rows, value_matrix, doc_ids))
    tokens_all = SEQUENCE_COUNT * SEQUENCE_LENGTH
    flat_rows = harvested.reshape(tokens_all, D)
    flat_expert = expert_ids.reshape(tokens_all)
    flat_slot = slot_ids.reshape(tokens_all)
    kept_token = flat_slot >= 0
    token_index = jnp.arange(tokens_all, dtype=jnp.int32)
    source_block = token_index // TOK_DEV
    slot_total = tokens_all // TOK_DEV * CAP
    padded_rows = jnp.concatenate([flat_rows, jnp.zeros((1, D), jnp.bfloat16)], axis=0)

    def one_expert(rebuilt_all, expert_index):
        mine = kept_token & (flat_expert == expert_index)
        place = jnp.where(mine, source_block * CAP + flat_slot, slot_total).astype(jnp.int32)
        table = jnp.full((slot_total,), tokens_all, jnp.int32).at[place].set(token_index, mode='drop')
        slot_rows = padded_rows[table]
        slot_live = table < tokens_all
        centered = (slot_rows.astype(jnp.float32) - dec_bias).astype(jnp.bfloat16)
        pre_act = jnp.dot(centered, enc_weight[expert_index], preferred_element_type=jnp.float32) + enc_bias[expert_index]
        latent = jnp.maximum(pre_act, jnp.float32(0.0)).astype(jnp.bfloat16)
        rebuilt = (jnp.dot(latent, dec_weight[expert_index], preferred_element_type=jnp.float32) + dec_bias).astype(jnp.bfloat16)
        residue = (rebuilt.astype(jnp.float32) - slot_rows.astype(jnp.float32)).astype(jnp.bfloat16)
        gated = jnp.where(slot_live[:, None], latent, jnp.zeros_like(latent))
        grad_one = jnp.dot(gated.T, residue, preferred_element_type=jnp.float32).astype(jnp.bfloat16)
        rebuilt_all = rebuilt_all.at[table].set(rebuilt)
        return (rebuilt_all, grad_one)
    start_rows = jnp.zeros((tokens_all + 1, D), jnp.bfloat16)
    rebuilt_all, dec_grad = lax.scan(one_expert, start_rows, jnp.arange(EXPERTS, dtype=jnp.int32))
    reconstruction = jnp.where(kept_token[:, None], rebuilt_all[:tokens_all], dec_bias.astype(jnp.bfloat16)[None, :])
    error_rows = (reconstruction.astype(jnp.float32) - flat_rows.astype(jnp.float32)).astype(jnp.bfloat16)
    return (harvested, reconstruction.reshape(SEQUENCE_COUNT, SEQUENCE_LENGTH, D), error_rows.reshape(SEQUENCE_COUNT, SEQUENCE_LENGTH, D), dec_grad)
```

```python
import math

import jax
import jax.numpy as jnp
from jax import lax
from jax.experimental import pallas as pl
from jax.experimental.pallas import tpu as pltpu
from jax.sharding import PartitionSpec as P

HEAD_DIMENSION = 128
MESH = pl.DeviceIdType.MESH
TILE = 128
EMPTY = 1e30


def widen(src, wide):
    rows = src.shape[0]

    def step(i, carry):
        at = pl.ds(pl.multiple_of(i * 384, 384), 384)
        wide[at, :] = src[at, :].astype(jnp.float32)
        return carry

    lax.fori_loop(0, rows // 384, step, 0)


def narrow(wide, dst):
    rows = dst.shape[0]

    def step(i, carry):
        at = pl.ds(pl.multiple_of(i * 384, 384), 384)
        dst[at, :] = wide[at, :].astype(jnp.bfloat16)
        return carry

    lax.fori_loop(0, rows // 384, step, 0)


def exchange_start(src, dst, send_sem, recv_sem, own_sem, chunk):
    seq_n, exp_n = lax.axis_size("seq"), lax.axis_size("exp")
    s, p = lax.axis_index("seq"), lax.axis_index("exp")
    me = s * exp_n + p
    mine = pl.ds(pl.multiple_of(me * chunk, chunk), chunk)

    def step(d, carry):
        to_s = lax.rem(s + d // exp_n, seq_n)
        to_p = lax.rem(p + lax.rem(d, exp_n), exp_n)
        other = to_s * exp_n + to_p
        pltpu.make_async_remote_copy(
            src_ref=src.at[pl.ds(pl.multiple_of(other * chunk, chunk), chunk)],
            dst_ref=dst.at[mine],
            send_sem=send_sem,
            recv_sem=recv_sem,
            device_id=(to_s, to_p),
            device_id_type=MESH,
        ).start()
        return carry

    own = pltpu.make_async_copy(src.at[mine], dst.at[mine], own_sem)
    own.start()
    lax.fori_loop(1, seq_n * exp_n, step, 0)


def exchange_wait(src, dst, send_sem, recv_sem, own_sem, chunk):
    devices_all = lax.axis_size("seq") * lax.axis_size("exp")
    pltpu.make_async_copy(src.at[pl.ds(0, chunk)], dst.at[pl.ds(0, chunk)], own_sem).wait()
    others = pl.ds(0, chunk * (devices_all - 1))
    pltpu.make_async_copy(src.at[others], dst.at[others], recv_sem).wait()
    pltpu.make_async_copy(src.at[others], dst.at[others], send_sem).wait()


def experts_kernel(
    h_ref, row_ref, col_ref, encw_hbm, encb_ref, decw_hbm, decb_ref,
    picked_ref, grad_ref,
    encw, decw, wide, send, recv, back, ret, slot_rows, centered, latent, gated, residue,
    weight_sem, own_sem, send_sem, recv_sem,
):
    seq_n, exp_n = lax.axis_size("seq"), lax.axis_size("exp")
    s, p = lax.axis_index("seq"), lax.axis_index("exp")
    devices_all = seq_n * exp_n
    tokens, width = h_ref.shape
    slots = slot_rows.shape[0]
    latents = latent.shape[1]
    lanes = width // TILE
    chunk = slots // devices_all * lanes
    barrier = pltpu.get_barrier_semaphore()

    def greet(d, carry):
        to_s = lax.rem(s + d // exp_n, seq_n)
        to_p = lax.rem(p + lax.rem(d, exp_n), exp_n)
        pl.semaphore_signal(barrier, inc=1, device_id=(to_s, to_p), device_id_type=MESH)
        return carry

    lax.fori_loop(1, devices_all, greet, 0)
    enc_copy = pltpu.make_async_copy(encw_hbm, encw, weight_sem.at[0])
    dec_copy = pltpu.make_async_copy(decw_hbm, decw, weight_sem.at[1])
    enc_copy.start()
    dec_copy.start()

    place = lax.broadcasted_iota(jnp.int32, (slots, tokens), 0) == row_ref[...]
    pick = jnp.where(place, 1.0, 0.0)
    free = (1.0 - jnp.sum(pick, axis=1, keepdims=True)) * EMPTY
    pick = pick.astype(jnp.bfloat16)
    for n in range(lanes // 2):
        rows = jnp.dot(
            pick, h_ref[:, 2 * n * TILE : 2 * (n + 1) * TILE], preferred_element_type=jnp.float32
        )
        if n == 0:
            rows = rows + free
        wide[pl.ds(2 * n, slots, stride=lanes), :] = rows[:, :TILE]
        wide[pl.ds(2 * n + 1, slots, stride=lanes), :] = rows[:, TILE:]
    narrow(wide, send)
    pl.semaphore_wait(barrier, devices_all - 1)
    exchange_start(send, recv, send_sem.at[0], recv_sem.at[0], own_sem.at[0], chunk)
    exchange_wait(send, recv, send_sem.at[0], recv_sem.at[0], own_sem.at[0], chunk)

    widen(recv, wide)
    live = wide[pl.ds(0, slots, stride=lanes), :][:, :1] < 0.5 * EMPTY
    for c in range(lanes):
        at = slice(c * TILE, (c + 1) * TILE)
        part = wide[pl.ds(c, slots, stride=lanes), :]
        if c < 2:
            part = jnp.where(live, part, 0.0)
        slot_rows[:, at] = part.astype(jnp.bfloat16)
        centered[:, at] = (part - decb_ref[:, at]).astype(jnp.bfloat16)
    enc_copy.wait()
    for n in range(latents // 256):
        at = slice(n * 256, (n + 1) * 256)
        pre = jnp.dot(centered[...], encw[:, at], preferred_element_type=jnp.float32)
        act = jnp.maximum(pre + encb_ref[:, at], 0.0)
        latent[:, at] = act.astype(jnp.bfloat16)
        gated[:, at] = jnp.where(live, act, 0.0).astype(jnp.bfloat16)
    dec_copy.wait()
    for n in range(lanes // 2):
        at = slice(2 * n * TILE, 2 * (n + 1) * TILE)
        rebuilt = jnp.dot(latent[...], decw[:, at], preferred_element_type=jnp.float32)
        rebuilt = (rebuilt + decb_ref[:, at]).astype(jnp.bfloat16).astype(jnp.float32)
        residue[:, at] = (rebuilt - slot_rows[:, at].astype(jnp.float32)).astype(jnp.bfloat16)
        wide[pl.ds(2 * n, slots, stride=lanes), :] = rebuilt[:, :TILE]
        wide[pl.ds(2 * n + 1, slots, stride=lanes), :] = rebuilt[:, TILE:]
    narrow(wide, back)
    exchange_start(back, ret, send_sem.at[1], recv_sem.at[1], own_sem.at[1], chunk)

    def grad_step(n, carry):
        at = pl.ds(pl.multiple_of(n * 256, 256), 256)
        grad_ref[at, :] = lax.dot_general(
            gated[:, at], residue[...], (((0,), (0,)), ((), ())),
            preferred_element_type=jnp.float32,
        ).astype(jnp.bfloat16)
        return carry

    lax.fori_loop(0, latents // 256, grad_step, 0)
    exchange_wait(back, ret, send_sem.at[1], recv_sem.at[1], own_sem.at[1], chunk)

    widen(ret, wide)
    for c in range(lanes):
        slot_rows[:, c * TILE : (c + 1) * TILE] = wide[pl.ds(c, slots, stride=lanes), :].astype(
            jnp.bfloat16
        )
    unplace = lax.broadcasted_iota(jnp.int32, (tokens, slots), 1) == col_ref[...]
    unpick = jnp.where(unplace, 1.0, 0.0).astype(jnp.bfloat16)
    for n in range(width // 256):
        at = slice(n * 256, (n + 1) * 256)
        picked_ref[:, at] = jnp.dot(
            unpick, slot_rows[:, at], preferred_element_type=jnp.float32
        ).astype(jnp.bfloat16)


def run_experts(harvested, target, enc_weight, enc_bias, dec_weight, dec_bias, slots):
    tokens, width = harvested.shape
    latents = enc_bias.shape[0]
    lanes = width // TILE
    vmem = pl.BlockSpec(memory_space=pltpu.VMEM)
    hbm = pl.BlockSpec(memory_space=pl.ANY)
    tiles = pltpu.VMEM((slots * lanes, TILE), jnp.bfloat16)
    return pl.pallas_call(
        experts_kernel,
        out_shape=(
            jax.ShapeDtypeStruct((tokens, width), jnp.bfloat16),
            jax.ShapeDtypeStruct((latents, width), jnp.bfloat16),
        ),
        in_specs=[vmem, vmem, vmem, hbm, vmem, hbm, vmem],
        out_specs=(vmem, vmem),
        scratch_shapes=[
            pltpu.VMEM((width, latents), jnp.bfloat16),
            pltpu.VMEM((latents, width), jnp.bfloat16),
            pltpu.VMEM((slots * lanes, TILE), jnp.float32),
            tiles, tiles, tiles, tiles,
            pltpu.VMEM((slots, width), jnp.bfloat16),
            pltpu.VMEM((slots, width), jnp.bfloat16),
            pltpu.VMEM((slots, latents), jnp.bfloat16),
            pltpu.VMEM((slots, latents), jnp.bfloat16),
            pltpu.VMEM((slots, width), jnp.bfloat16),
            pltpu.SemaphoreType.DMA((2,)),
            pltpu.SemaphoreType.DMA((2,)),
            pltpu.SemaphoreType.DMA((2,)),
            pltpu.SemaphoreType.DMA((2,)),
        ],
        compiler_params=pltpu.CompilerParams(
            collective_id=0, has_side_effects=True, vmem_limit_bytes=48 * 2**20
        ),
    )(
        harvested, target[None, :], target[:, None], enc_weight, enc_bias[None, :], dec_weight,
        dec_bias[None, :],
    )


masked_score = -1e30


def attend_block(query_block, key_part, value_part, visible, score_scale):
    scores = (
        jnp.einsum("qhd,kd->hqk", query_block, key_part, preferred_element_type=jnp.float32)
        * score_scale
    )
    scores = jnp.where(visible[None, :, :], scores, masked_score)
    highest = jnp.max(scores, axis=2, keepdims=True)
    weights = jnp.exp(scores - highest)
    normed = (weights / jnp.sum(weights, axis=2, keepdims=True)).astype(jnp.bfloat16)
    mixed = jnp.einsum("hqk,kd->qhd", normed, value_part, preferred_element_type=jnp.float32)
    return mixed.astype(jnp.bfloat16)


def shards(
    query_rows,
    key_rows,
    value_matrix,
    doc_ids,
    out_weight,
    enc_weight,
    enc_bias,
    dec_weight,
    dec_bias,
    expert_ids,
    slot_ids,
):
    local_tokens = query_rows.shape[1]
    seq_groups = lax.axis_size("seq")
    exp_groups = lax.axis_size("exp")
    devices_all = seq_groups * exp_groups
    query_heads = query_rows.shape[2] // HEAD_DIMENSION
    kv_heads = key_rows.shape[2] // HEAD_DIMENSION
    heads_here = query_heads // seq_groups
    kv_share = seq_groups // kv_heads
    query_local = query_rows[0].reshape(local_tokens, seq_groups, heads_here * HEAD_DIMENSION)
    paired = jnp.concatenate(
        [
            key_rows[0].reshape(local_tokens, kv_heads, HEAD_DIMENSION),
            value_matrix[0].reshape(local_tokens, kv_heads, HEAD_DIMENSION),
        ],
        axis=2,
    )
    paired = jnp.repeat(paired, kv_share, axis=1)
    query_all, paired_all = (
        lax.all_to_all(query_local, "seq", split_axis=1, concat_axis=0, tiled=True),
        lax.all_to_all(paired, "seq", split_axis=1, concat_axis=0, tiled=True),
    )
    span_length = local_tokens * seq_groups
    query_all = query_all.reshape(span_length, heads_here, HEAD_DIMENSION)
    key_all = paired_all[:, 0, :HEAD_DIMENSION]
    value_all = paired_all[:, 0, HEAD_DIMENSION:]
    doc_row = doc_ids[0]
    positions = jnp.arange(span_length)
    block_rows = 512
    score_scale = 1.0 / math.sqrt(HEAD_DIMENSION)
    pieces_out = []
    for row_start in range(0, span_length, block_rows):
        row_stop = row_start + block_rows
        visible = (positions[row_start:row_stop, None] >= positions[None, :row_stop]) & (
            doc_row[row_start:row_stop, None] == doc_row[None, :row_stop]
        )
        mixed = attend_block(
            query_all[row_start:row_stop],
            key_all[:row_stop],
            value_all[:row_stop],
            visible,
            score_scale,
        )
        pieces_out.append(mixed.reshape(block_rows, heads_here * HEAD_DIMENSION))
    attended = jnp.concatenate(pieces_out, axis=0)
    heads_back = lax.all_to_all(
        attended.reshape(seq_groups, local_tokens, heads_here * HEAD_DIMENSION),
        "seq",
        split_axis=0,
        concat_axis=2,
        tiled=True,
    )
    head_features = heads_back[0]
    projected = jnp.dot(
        head_features,
        lax.all_gather(out_weight, ("seq", "exp"), axis=0, tiled=True),
        preferred_element_type=jnp.float32,
    )
    harvested = projected.astype(jnp.bfloat16)
    local_experts = enc_weight.shape[0]
    experts_all = local_experts * devices_all
    capacity = 2 * local_tokens // experts_all
    expert_here = expert_ids[0]
    slot_here = slot_ids[0]
    kept_token = slot_here >= 0
    slot_count = experts_all * capacity
    target = jnp.where(kept_token, expert_here * capacity + slot_here, slot_count)
    picked_rows, dec_grad = run_experts(
        harvested, target, enc_weight[0], enc_bias[0], dec_weight[0], dec_bias, slot_count
    )
    reconstruction = jnp.where(
        kept_token[:, None], picked_rows, dec_bias.astype(jnp.bfloat16)[None, :]
    )
    error_rows = (reconstruction.astype(jnp.float32) - harvested.astype(jnp.float32)).astype(
        jnp.bfloat16
    )
    return (harvested[None], reconstruction[None], error_rows[None], dec_grad[None])


def solution(mesh):
    return jax.shard_map(
        shards,
        mesh=mesh,
        in_specs=(
            P("exp", "seq", None),
            P("exp", "seq", None),
            P("exp", "seq", None),
            P("exp", None),
            P(("seq", "exp"), None),
            P(("seq", "exp"), None, None),
            P(("seq", "exp"), None),
            P(("seq", "exp"), None, None),
            P(),
            P("exp", "seq"),
            P("exp", "seq"),
        ),
        out_specs=(
            P("exp", "seq", None),
            P("exp", "seq", None),
            P("exp", "seq", None),
            P(("seq", "exp"), None, None),
        ),
        check_vma=False,
    )
```

```python
import math

import jax
import jax.numpy as jnp
from jax import lax
from jax.experimental import pallas as pl
from jax.experimental.pallas import tpu as pltpu
from jax.sharding import PartitionSpec as P

HEAD_DIMENSION = 128
MESH = pl.DeviceIdType.MESH
TILE = 128
EMPTY = 1e30
PARTS = ((0, 384), (384, 256), (640, 384))
ORDERS = ("xyz", "yzx", "zxy")


def attention_kernel(
    q_ref, k_ref, v_ref, doc_col, doc_row, w_ref,
    out_ref,
    kv, w_a, w_b, w_c, attended, bias, result, half_in, send_sem, recv_sem,
):
    s, p = lax.axis_index("seq"), lax.axis_index("exp")
    place = {"x": s // 2, "y": p // 4, "z": lax.rem(p, 4)}
    core = lax.rem(s, 2)
    tokens = q_ref.shape[0]
    kv_width = k_ref.shape[1]
    span = kv.shape[0] * tokens
    half = out_ref.shape[1] // 2
    scale = 1.0 / math.sqrt(HEAD_DIMENSION)
    parts = (w_a, w_b, w_c)
    partner = (2 * place["x"] + 1 - core, p)

    def beside(axis, step):
        at = dict(place)
        at[axis] = lax.rem(at[axis] + step + 4, 4)
        return (2 * at["x"] + core, 4 * at["y"] + at["z"])

    peers = [partner] + [beside(axis, step) for axis in "xyz" for step in (1, -1)]
    barrier = pltpu.get_barrier_semaphore()
    for peer in peers:
        pl.semaphore_signal(barrier, inc=1, device_id=peer, device_id_type=MESH)

    started = []

    def send(src, dst, peer):
        copy = pltpu.make_async_remote_copy(
            src_ref=src,
            dst_ref=dst,
            send_sem=send_sem.at[len(started)],
            recv_sem=recv_sem.at[len(started)],
            device_id=peer,
            device_id_type=MESH,
        )
        started.append(copy)
        copy.start()
        return copy

    def arrive(copies):
        for copy in copies:
            copy.wait_recv()

    kv[s, :, :kv_width] = k_ref[...]
    kv[s, :, kv_width:] = v_ref[...]
    for (first, wide), buffer in zip(PARTS, parts):
        columns = pl.ds(pl.multiple_of(core * half + first, TILE), wide)
        buffer[place["x"], core, place["y"], place["z"]] = w_ref[:, columns]
    pl.semaphore_wait(barrier, len(peers))

    kv_near = [send(kv.at[s], kv.at[s], beside("x", step)) for step in (1, -1)]
    kv_pair = [send(kv.at[s], kv.at[s], partner)]
    w_pair = []
    for (first, wide), buffer in zip(PARTS, parts):
        columns = pl.ds(pl.multiple_of((1 - core) * half + first, TILE), wide)
        w_pair.append(
            send(
                w_ref.at[:, columns],
                buffer.at[place["x"], core, place["y"], place["z"]],
                partner,
            )
        )

    def block(part, stage, offset, rows):
        order = ORDERS[part]
        at = {}
        for i, axis in enumerate(order):
            if i < stage:
                at[axis] = pl.ds(0, 4)
            elif i == stage:
                at[axis] = pl.ds(lax.rem(place[axis] + offset + 4, 4), 1)
            else:
                at[axis] = pl.ds(place[axis], 1)
        return parts[part].at[at["x"], rows, at["y"], at["z"]]

    def stage_near(stage):
        copies = []
        for part in range(3):
            axis = ORDERS[part][stage]
            for step in (1, -1):
                view = block(part, stage, 0, pl.ds(0, 2))
                copies.append(send(view, view, beside(axis, step)))
        return copies

    def stage_far(stage):
        copies = []
        for part in range(3):
            axis = ORDERS[part][stage]
            for step, row in ((1, 0), (-1, 1)):
                view = block(part, stage, -step, pl.ds(row, 1))
                copies.append(send(view, view, beside(axis, step)))
        return copies

    def kv_far():
        copies, pair = [], []
        for step, first in ((1, 0), (-1, tokens // 2)):
            origin = 2 * lax.rem(place["x"] - step + 4, 4) + core
            view = kv.at[origin, pl.ds(first, tokens // 2)]
            copies.append(send(view, view, beside("x", step)))
        for step in (1, -1):
            view = kv.at[2 * lax.rem(place["x"] - step + 4, 4) + core]
            pair.append(send(view, view, partner))
        return copies, pair

    arrive(w_pair)
    near = stage_near(0)
    rows_at = s * tokens + lax.broadcasted_iota(jnp.int32, (tokens, span), 0)
    keys_at = lax.broadcasted_iota(jnp.int32, (tokens, span), 1)
    visible = (rows_at >= keys_at) & (doc_col[...] == doc_row[...])
    bias[...] = jnp.where(visible, 0.0, -EMPTY)
    arrive(near)
    far = stage_far(0)
    arrive(far)
    near = stage_near(1)
    arrive(kv_near)
    kv_across, pair = kv_far()
    kv_pair += pair
    arrive(near)
    far = stage_far(1)
    arrive(far)
    near = stage_near(2)
    arrive(kv_across)
    view = kv.at[2 * lax.rem(place["x"] + 2, 4) + core]
    kv_pair.append(send(view, view, partner))
    arrive(kv_pair)

    heads = q_ref.shape[1] // HEAD_DIMENSION
    group = heads // (kv_width // HEAD_DIMENSION)

    def attend(first, last, blocks):
        keys = blocks * tokens

        def one_head(h, carry):
            g = h // group
            q_at = pl.ds(pl.multiple_of(h * HEAD_DIMENSION, HEAD_DIMENSION), HEAD_DIMENSION)
            k_at = pl.ds(pl.multiple_of(g * HEAD_DIMENSION, HEAD_DIMENSION), HEAD_DIMENSION)
            v_at = pl.ds(
                pl.multiple_of(kv_width + g * HEAD_DIMENSION, HEAD_DIMENSION), HEAD_DIMENSION
            )
            key_part = kv[:blocks, :, k_at].reshape(keys, HEAD_DIMENSION)
            value_part = kv[:blocks, :, v_at].reshape(keys, HEAD_DIMENSION)
            scores = lax.dot_general(
                q_ref[:, q_at], key_part, (((1,), (1,)), ((), ())),
                preferred_element_type=jnp.float32,
            )
            scores = scores + bias[:, :keys]
            highest = jnp.max(scores, axis=1, keepdims=True)
            weights = jnp.exp2((scores - highest) * (scale * math.log2(math.e)))
            total = jnp.sum(weights, axis=1, keepdims=True)
            mixed = jnp.dot(
                weights.astype(jnp.bfloat16), value_part, preferred_element_type=jnp.float32
            )
            attended[core, :, q_at] = (mixed / total).astype(jnp.bfloat16)
            return carry

        lax.fori_loop(first, last, one_head, 0)

    def attend_heads(first, last):
        for chips in range(1, 5):

            @pl.when(place["x"] == chips - 1)
            def _():
                attend(first, last, 2 * chips)

        columns = pl.ds(first * HEAD_DIMENSION, (last - first) * HEAD_DIMENSION)
        view = attended.at[core, :, columns]
        return send(view, view, partner)

    across = [attend_heads(0, heads // 2)]
    arrive(near)
    far = stage_far(2)
    across.append(attend_heads(heads // 2, heads))
    arrive(far)
    arrive(across)

    rows = attended.shape[1] * 2
    for (first, wide), buffer in zip(PARTS, parts):
        for n in range(0, wide, TILE):
            weight = buffer[:, :, :, :, :, n : n + TILE].reshape(heads * HEAD_DIMENSION, TILE)
            both = jnp.dot(
                attended[...].reshape(rows, heads * HEAD_DIMENSION),
                weight,
                preferred_element_type=jnp.float32,
            )
            result[:, :, first + n : first + n + TILE] = both.astype(jnp.bfloat16).reshape(
                2, tokens, TILE
            )
    back = send(result.at[1 - core], half_in, partner)
    out_ref[:, pl.ds(pl.multiple_of(core * half, half), half)] = result[core]
    arrive([back])
    out_ref[:, pl.ds(pl.multiple_of((1 - core) * half, half), half)] = half_in[...]
    for copy in started:
        copy.wait_send()


def run_attention(query, key, value, doc_mine, doc_all, out_weight, seq_groups):
    tokens, q_width = query.shape
    kv_width = key.shape[1]
    span = tokens * seq_groups
    rows, width = out_weight.shape
    vmem = pl.BlockSpec(memory_space=pltpu.VMEM)
    copies = 64
    return pl.pallas_call(
        attention_kernel,
        out_shape=jax.ShapeDtypeStruct((tokens, width), jnp.bfloat16),
        in_specs=[vmem] * 6,
        out_specs=vmem,
        scratch_shapes=[
            pltpu.VMEM((seq_groups, tokens, 2 * kv_width), jnp.bfloat16),
            *[pltpu.VMEM((4, 2, 4, 4, rows, wide), jnp.bfloat16) for _, wide in PARTS],
            pltpu.VMEM((2, tokens, q_width), jnp.bfloat16),
            pltpu.VMEM((tokens, span), jnp.float32),
            pltpu.VMEM((2, tokens, width // 2), jnp.bfloat16),
            pltpu.VMEM((tokens, width // 2), jnp.bfloat16),
            pltpu.SemaphoreType.DMA((copies,)),
            pltpu.SemaphoreType.DMA((copies,)),
        ],
        compiler_params=pltpu.CompilerParams(
            collective_id=1, has_side_effects=True, vmem_limit_bytes=48 * 2**20
        ),
    )(query, key, value, doc_mine[:, None], doc_all[None, :], out_weight)


def widen(src, wide):
    rows = src.shape[0]

    def step(i, carry):
        at = pl.ds(pl.multiple_of(i * 384, 384), 384)
        wide[at, :] = src[at, :].astype(jnp.float32)
        return carry

    lax.fori_loop(0, rows // 384, step, 0)


def narrow(wide, dst):
    rows = dst.shape[0]

    def step(i, carry):
        at = pl.ds(pl.multiple_of(i * 384, 384), 384)
        dst[at, :] = wide[at, :].astype(jnp.bfloat16)
        return carry

    lax.fori_loop(0, rows // 384, step, 0)


def exchange_start(src, dst, send_sem, recv_sem, own_sem, chunk):
    seq_n, exp_n = lax.axis_size("seq"), lax.axis_size("exp")
    s, p = lax.axis_index("seq"), lax.axis_index("exp")
    me = s * exp_n + p
    mine = pl.ds(pl.multiple_of(me * chunk, chunk), chunk)

    def step(d, carry):
        to_s = lax.rem(s + d // exp_n, seq_n)
        to_p = lax.rem(p + lax.rem(d, exp_n), exp_n)
        other = to_s * exp_n + to_p
        pltpu.make_async_remote_copy(
            src_ref=src.at[pl.ds(pl.multiple_of(other * chunk, chunk), chunk)],
            dst_ref=dst.at[mine],
            send_sem=send_sem,
            recv_sem=recv_sem,
            device_id=(to_s, to_p),
            device_id_type=MESH,
        ).start()
        return carry

    own = pltpu.make_async_copy(src.at[mine], dst.at[mine], own_sem)
    own.start()
    lax.fori_loop(1, seq_n * exp_n, step, 0)


def exchange_wait(src, dst, send_sem, recv_sem, own_sem, chunk):
    devices_all = lax.axis_size("seq") * lax.axis_size("exp")
    pltpu.make_async_copy(src.at[pl.ds(0, chunk)], dst.at[pl.ds(0, chunk)], own_sem).wait()
    others = pl.ds(0, chunk * (devices_all - 1))
    pltpu.make_async_copy(src.at[others], dst.at[others], recv_sem).wait()
    pltpu.make_async_copy(src.at[others], dst.at[others], send_sem).wait()


def experts_kernel(
    h_ref, row_ref, col_ref, encw_hbm, encb_ref, decw_hbm, decb_ref,
    picked_ref, grad_ref,
    encw, decw, wide, send, recv, back, ret, slot_rows, centered, latent, gated, residue,
    weight_sem, own_sem, send_sem, recv_sem,
):
    seq_n, exp_n = lax.axis_size("seq"), lax.axis_size("exp")
    s, p = lax.axis_index("seq"), lax.axis_index("exp")
    devices_all = seq_n * exp_n
    tokens, width = h_ref.shape
    slots = slot_rows.shape[0]
    latents = latent.shape[1]
    lanes = width // TILE
    chunk = slots // devices_all * lanes
    barrier = pltpu.get_barrier_semaphore()

    def greet(d, carry):
        to_s = lax.rem(s + d // exp_n, seq_n)
        to_p = lax.rem(p + lax.rem(d, exp_n), exp_n)
        pl.semaphore_signal(barrier, inc=1, device_id=(to_s, to_p), device_id_type=MESH)
        return carry

    lax.fori_loop(1, devices_all, greet, 0)
    enc_copy = pltpu.make_async_copy(encw_hbm, encw, weight_sem.at[0])
    dec_copy = pltpu.make_async_copy(decw_hbm, decw, weight_sem.at[1])
    enc_copy.start()
    dec_copy.start()

    place = lax.broadcasted_iota(jnp.int32, (slots, tokens), 0) == row_ref[...]
    pick = jnp.where(place, 1.0, 0.0)
    free = (1.0 - jnp.sum(pick, axis=1, keepdims=True)) * EMPTY
    pick = pick.astype(jnp.bfloat16)
    for n in range(lanes // 2):
        rows = jnp.dot(
            pick, h_ref[:, 2 * n * TILE : 2 * (n + 1) * TILE], preferred_element_type=jnp.float32
        )
        if n == 0:
            rows = rows + free
        wide[pl.ds(2 * n, slots, stride=lanes), :] = rows[:, :TILE]
        wide[pl.ds(2 * n + 1, slots, stride=lanes), :] = rows[:, TILE:]
    narrow(wide, send)
    pl.semaphore_wait(barrier, devices_all - 1)
    exchange_start(send, recv, send_sem.at[0], recv_sem.at[0], own_sem.at[0], chunk)
    exchange_wait(send, recv, send_sem.at[0], recv_sem.at[0], own_sem.at[0], chunk)

    widen(recv, wide)
    live = wide[pl.ds(0, slots, stride=lanes), :][:, :1] < 0.5 * EMPTY
    for c in range(lanes):
        at = slice(c * TILE, (c + 1) * TILE)
        part = wide[pl.ds(c, slots, stride=lanes), :]
        if c < 2:
            part = jnp.where(live, part, 0.0)
        slot_rows[:, at] = part.astype(jnp.bfloat16)
        centered[:, at] = (part - decb_ref[:, at]).astype(jnp.bfloat16)
    enc_copy.wait()
    for n in range(latents // 256):
        at = slice(n * 256, (n + 1) * 256)
        pre = jnp.dot(centered[...], encw[:, at], preferred_element_type=jnp.float32)
        act = jnp.maximum(pre + encb_ref[:, at], 0.0)
        latent[:, at] = act.astype(jnp.bfloat16)
        gated[:, at] = jnp.where(live, act, 0.0).astype(jnp.bfloat16)
    dec_copy.wait()
    for n in range(lanes // 2):
        at = slice(2 * n * TILE, 2 * (n + 1) * TILE)
        rebuilt = jnp.dot(latent[...], decw[:, at], preferred_element_type=jnp.float32)
        rebuilt = (rebuilt + decb_ref[:, at]).astype(jnp.bfloat16).astype(jnp.float32)
        residue[:, at] = (rebuilt - slot_rows[:, at].astype(jnp.float32)).astype(jnp.bfloat16)
        wide[pl.ds(2 * n, slots, stride=lanes), :] = rebuilt[:, :TILE]
        wide[pl.ds(2 * n + 1, slots, stride=lanes), :] = rebuilt[:, TILE:]
    narrow(wide, back)
    exchange_start(back, ret, send_sem.at[1], recv_sem.at[1], own_sem.at[1], chunk)

    def grad_step(n, carry):
        at = pl.ds(pl.multiple_of(n * 256, 256), 256)
        grad_ref[at, :] = lax.dot_general(
            gated[:, at], residue[...], (((0,), (0,)), ((), ())),
            preferred_element_type=jnp.float32,
        ).astype(jnp.bfloat16)
        return carry

    lax.fori_loop(0, latents // 256, grad_step, 0)
    exchange_wait(back, ret, send_sem.at[1], recv_sem.at[1], own_sem.at[1], chunk)

    widen(ret, wide)
    for c in range(lanes):
        slot_rows[:, c * TILE : (c + 1) * TILE] = wide[pl.ds(c, slots, stride=lanes), :].astype(
            jnp.bfloat16
        )
    unplace = lax.broadcasted_iota(jnp.int32, (tokens, slots), 1) == col_ref[...]
    unpick = jnp.where(unplace, 1.0, 0.0).astype(jnp.bfloat16)
    for n in range(width // 256):
        at = slice(n * 256, (n + 1) * 256)
        picked_ref[:, at] = jnp.dot(
            unpick, slot_rows[:, at], preferred_element_type=jnp.float32
        ).astype(jnp.bfloat16)


def run_experts(harvested, target, enc_weight, enc_bias, dec_weight, dec_bias, slots):
    tokens, width = harvested.shape
    latents = enc_bias.shape[0]
    lanes = width // TILE
    vmem = pl.BlockSpec(memory_space=pltpu.VMEM)
    hbm = pl.BlockSpec(memory_space=pl.ANY)
    tiles = pltpu.VMEM((slots * lanes, TILE), jnp.bfloat16)
    return pl.pallas_call(
        experts_kernel,
        out_shape=(
            jax.ShapeDtypeStruct((tokens, width), jnp.bfloat16),
            jax.ShapeDtypeStruct((latents, width), jnp.bfloat16),
        ),
        in_specs=[vmem, vmem, vmem, hbm, vmem, hbm, vmem],
        out_specs=(vmem, vmem),
        scratch_shapes=[
            pltpu.VMEM((width, latents), jnp.bfloat16),
            pltpu.VMEM((latents, width), jnp.bfloat16),
            pltpu.VMEM((slots * lanes, TILE), jnp.float32),
            tiles, tiles, tiles, tiles,
            pltpu.VMEM((slots, width), jnp.bfloat16),
            pltpu.VMEM((slots, width), jnp.bfloat16),
            pltpu.VMEM((slots, latents), jnp.bfloat16),
            pltpu.VMEM((slots, latents), jnp.bfloat16),
            pltpu.VMEM((slots, width), jnp.bfloat16),
            pltpu.SemaphoreType.DMA((2,)),
            pltpu.SemaphoreType.DMA((2,)),
            pltpu.SemaphoreType.DMA((2,)),
            pltpu.SemaphoreType.DMA((2,)),
        ],
        compiler_params=pltpu.CompilerParams(
            collective_id=0, has_side_effects=True, vmem_limit_bytes=48 * 2**20
        ),
    )(
        harvested, target[None, :], target[:, None], enc_weight, enc_bias[None, :], dec_weight,
        dec_bias[None, :],
    )


def shards(
    query_rows,
    key_rows,
    value_matrix,
    doc_ids,
    out_weight,
    enc_weight,
    enc_bias,
    dec_weight,
    dec_bias,
    expert_ids,
    slot_ids,
):
    local_tokens = query_rows.shape[1]
    seq_groups = lax.axis_size("seq")
    exp_groups = lax.axis_size("exp")
    devices_all = seq_groups * exp_groups
    doc_row = doc_ids[0]
    doc_mine = lax.dynamic_slice_in_dim(
        doc_row, lax.axis_index("seq") * local_tokens, local_tokens
    )
    harvested = run_attention(
        query_rows[0], key_rows[0], value_matrix[0], doc_mine, doc_row, out_weight, seq_groups
    )
    local_experts = enc_weight.shape[0]
    experts_all = local_experts * devices_all
    capacity = 2 * local_tokens // experts_all
    expert_here = expert_ids[0]
    slot_here = slot_ids[0]
    kept_token = slot_here >= 0
    slot_count = experts_all * capacity
    target = jnp.where(kept_token, expert_here * capacity + slot_here, slot_count)
    picked_rows, dec_grad = run_experts(
        harvested, target, enc_weight[0], enc_bias[0], dec_weight[0], dec_bias, slot_count
    )
    reconstruction = jnp.where(
        kept_token[:, None], picked_rows, dec_bias.astype(jnp.bfloat16)[None, :]
    )
    error_rows = (reconstruction.astype(jnp.float32) - harvested.astype(jnp.float32)).astype(
        jnp.bfloat16
    )
    return (harvested[None], reconstruction[None], error_rows[None], dec_grad[None])


def solution(mesh):
    return jax.shard_map(
        shards,
        mesh=mesh,
        in_specs=(
            P("exp", "seq", None),
            P("exp", "seq", None),
            P("exp", "seq", None),
            P("exp", None),
            P(("seq", "exp"), None),
            P(("seq", "exp"), None, None),
            P(("seq", "exp"), None),
            P(("seq", "exp"), None, None),
            P(),
            P("exp", "seq"),
            P("exp", "seq"),
        ),
        out_specs=(
            P("exp", "seq", None),
            P("exp", "seq", None),
            P("exp", "seq", None),
            P(("seq", "exp"), None, None),
        ),
        check_vma=False,
    )
```

```python
import math

import jax
import jax.numpy as jnp
from jax import lax
from jax.experimental import pallas as pl
from jax.experimental.pallas import tpu as pltpu
from jax.sharding import PartitionSpec as P

HEAD_DIMENSION = 128
MESH = pl.DeviceIdType.MESH
TILE = 128
EMPTY = 1e30
PARTS = ((0, 384), (384, 256), (640, 384))
ORDERS = ("xyz", "yzx", "zxy")


def attention_kernel(
    q_ref, k_ref, v_ref, doc_col, doc_row, w_ref,
    out_ref,
    kv, w_a, w_b, w_c, attended, bias, result, half_in, send_sem, recv_sem,
):
    s, p = lax.axis_index("seq"), lax.axis_index("exp")
    place = {"x": s // 2, "y": p // 4, "z": lax.rem(p, 4)}
    core = lax.rem(s, 2)
    tokens = q_ref.shape[0]
    kv_width = k_ref.shape[1]
    span = kv.shape[0] * tokens
    half = out_ref.shape[1] // 2
    scale = 1.0 / math.sqrt(HEAD_DIMENSION)
    parts = (w_a, w_b, w_c)
    partner = (2 * place["x"] + 1 - core, p)

    def beside(axis, step):
        at = dict(place)
        at[axis] = lax.rem(at[axis] + step + 4, 4)
        return (2 * at["x"] + core, 4 * at["y"] + at["z"])

    peers = [partner] + [beside(axis, step) for axis in "xyz" for step in (1, -1)]
    barrier = pltpu.get_barrier_semaphore()
    for peer in peers:
        pl.semaphore_signal(barrier, inc=1, device_id=peer, device_id_type=MESH)

    started = []

    def send(src, dst, peer):
        copy = pltpu.make_async_remote_copy(
            src_ref=src,
            dst_ref=dst,
            send_sem=send_sem.at[len(started)],
            recv_sem=recv_sem.at[len(started)],
            device_id=peer,
            device_id_type=MESH,
        )
        started.append(copy)
        copy.start()
        return copy

    def arrive(copies):
        for copy in copies:
            copy.wait_recv()

    kv[s, :, :kv_width] = k_ref[...]
    kv[s, :, kv_width:] = v_ref[...]
    for (first, wide), buffer in zip(PARTS, parts):
        columns = pl.ds(pl.multiple_of(core * half + first, TILE), wide)
        buffer[place["x"], core, place["y"], place["z"]] = w_ref[:, columns]
    pl.semaphore_wait(barrier, len(peers))

    kv_near = [send(kv.at[s], kv.at[s], beside("x", step)) for step in (1, -1)]
    kv_pair = [send(kv.at[s], kv.at[s], partner)]
    w_pair = []
    for (first, wide), buffer in zip(PARTS, parts):
        columns = pl.ds(pl.multiple_of((1 - core) * half + first, TILE), wide)
        w_pair.append(
            send(
                w_ref.at[:, columns],
                buffer.at[place["x"], core, place["y"], place["z"]],
                partner,
            )
        )

    def block(part, stage, offset, rows):
        order = ORDERS[part]
        at = {}
        for i, axis in enumerate(order):
            if i < stage:
                at[axis] = pl.ds(0, 4)
            elif i == stage:
                at[axis] = pl.ds(lax.rem(place[axis] + offset + 4, 4), 1)
            else:
                at[axis] = pl.ds(place[axis], 1)
        return parts[part].at[at["x"], rows, at["y"], at["z"]]

    def stage_near(stage):
        copies = []
        for part in range(3):
            axis = ORDERS[part][stage]
            for step in (1, -1):
                view = block(part, stage, 0, pl.ds(0, 2))
                copies.append(send(view, view, beside(axis, step)))
        return copies

    def stage_far(stage):
        copies = []
        for part in range(3):
            axis = ORDERS[part][stage]
            for step, row in ((1, 0), (-1, 1)):
                view = block(part, stage, -step, pl.ds(row, 1))
                copies.append(send(view, view, beside(axis, step)))
        return copies

    def kv_far():
        copies, pair = [], []
        for step, first in ((1, 0), (-1, tokens // 2)):
            origin = 2 * lax.rem(place["x"] - step + 4, 4) + core
            view = kv.at[origin, pl.ds(first, tokens // 2)]
            copies.append(send(view, view, beside("x", step)))
        for step in (1, -1):
            view = kv.at[2 * lax.rem(place["x"] - step + 4, 4) + core]
            pair.append(send(view, view, partner))
        return copies, pair

    arrive(w_pair)
    near = stage_near(0)
    rows_at = s * tokens + lax.broadcasted_iota(jnp.int32, (tokens, span), 0)
    keys_at = lax.broadcasted_iota(jnp.int32, (tokens, span), 1)
    visible = (rows_at >= keys_at) & (doc_col[...] == doc_row[...])
    bias[...] = jnp.where(visible, 0.0, -EMPTY)
    arrive(near)
    far = stage_far(0)
    arrive(far)
    near = stage_near(1)
    arrive(kv_near)
    kv_across, pair = kv_far()
    kv_pair += pair
    arrive(near)
    far = stage_far(1)
    arrive(far)
    near = stage_near(2)
    arrive(kv_across)
    view = kv.at[2 * lax.rem(place["x"] + 2, 4) + core]
    kv_pair.append(send(view, view, partner))
    arrive(kv_pair)

    heads = q_ref.shape[1] // HEAD_DIMENSION
    group = heads // (kv_width // HEAD_DIMENSION)

    def attend(first, last, blocks):
        keys = blocks * tokens

        def one_head(h, carry):
            g = h // group
            q_at = pl.ds(pl.multiple_of(h * HEAD_DIMENSION, HEAD_DIMENSION), HEAD_DIMENSION)
            k_at = pl.ds(pl.multiple_of(g * HEAD_DIMENSION, HEAD_DIMENSION), HEAD_DIMENSION)
            v_at = pl.ds(
                pl.multiple_of(kv_width + g * HEAD_DIMENSION, HEAD_DIMENSION), HEAD_DIMENSION
            )
            key_part = kv[:blocks, :, k_at].reshape(keys, HEAD_DIMENSION)
            value_part = kv[:blocks, :, v_at].reshape(keys, HEAD_DIMENSION)
            scores = lax.dot_general(
                q_ref[:, q_at], key_part, (((1,), (1,)), ((), ())),
                preferred_element_type=jnp.float32,
            )
            scores = scores + bias[:, :keys]
            highest = jnp.max(scores, axis=1, keepdims=True)
            weights = jnp.exp2((scores - highest) * (scale * math.log2(math.e)))
            total = jnp.sum(weights, axis=1, keepdims=True)
            mixed = jnp.dot(
                weights.astype(jnp.bfloat16), value_part, preferred_element_type=jnp.float32
            )
            attended[core, :, q_at] = (mixed / total).astype(jnp.bfloat16)
            return carry

        lax.fori_loop(first, last, one_head, 0)

    def attend_heads(first, last):
        for chips in range(1, 5):

            @pl.when(place["x"] == chips - 1)
            def _():
                attend(first, last, 2 * chips)

        columns = pl.ds(first * HEAD_DIMENSION, (last - first) * HEAD_DIMENSION)
        view = attended.at[core, :, columns]
        return send(view, view, partner)

    across = [attend_heads(0, heads // 2)]
    arrive(near)
    far = stage_far(2)
    across.append(attend_heads(heads // 2, heads))
    arrive(far)
    arrive(across)

    rows = attended.shape[1] * 2
    for (first, wide), buffer in zip(PARTS, parts):
        for n in range(0, wide, TILE):
            weight = buffer[:, :, :, :, :, n : n + TILE].reshape(heads * HEAD_DIMENSION, TILE)
            both = jnp.dot(
                attended[...].reshape(rows, heads * HEAD_DIMENSION),
                weight,
                preferred_element_type=jnp.float32,
            )
            result[:, :, first + n : first + n + TILE] = both.astype(jnp.bfloat16).reshape(
                2, tokens, TILE
            )
    back = send(result.at[1 - core], half_in, partner)
    out_ref[:, pl.ds(pl.multiple_of(core * half, half), half)] = result[core]
    arrive([back])
    out_ref[:, pl.ds(pl.multiple_of((1 - core) * half, half), half)] = half_in[...]
    for copy in started:
        copy.wait_send()


def run_attention(query, key, value, doc_mine, doc_all, out_weight, seq_groups):
    tokens, q_width = query.shape
    kv_width = key.shape[1]
    span = tokens * seq_groups
    rows, width = out_weight.shape
    vmem = pl.BlockSpec(memory_space=pltpu.VMEM)
    copies = 64
    return pl.pallas_call(
        attention_kernel,
        out_shape=jax.ShapeDtypeStruct((tokens, width), jnp.bfloat16),
        in_specs=[vmem] * 6,
        out_specs=vmem,
        scratch_shapes=[
            pltpu.VMEM((seq_groups, tokens, 2 * kv_width), jnp.bfloat16),
            *[pltpu.VMEM((4, 2, 4, 4, rows, wide), jnp.bfloat16) for _, wide in PARTS],
            pltpu.VMEM((2, tokens, q_width), jnp.bfloat16),
            pltpu.VMEM((tokens, span), jnp.float32),
            pltpu.VMEM((2, tokens, width // 2), jnp.bfloat16),
            pltpu.VMEM((tokens, width // 2), jnp.bfloat16),
            pltpu.SemaphoreType.DMA((copies,)),
            pltpu.SemaphoreType.DMA((copies,)),
        ],
        compiler_params=pltpu.CompilerParams(
            collective_id=1, has_side_effects=True, vmem_limit_bytes=48 * 2**20
        ),
    )(query, key, value, doc_mine[:, None], doc_all[None, :], out_weight)


GROUPS = 4


def widen(src, wide, first, rows):
    def step(i, carry):
        at = pl.ds(pl.multiple_of(first + i * 384, 384), 384)
        wide[at, :] = src[at, :].astype(jnp.float32)
        return carry

    lax.fori_loop(0, rows // 384, step, 0)


def narrow(wide, dst, first, rows):
    def step(i, carry):
        at = pl.ds(pl.multiple_of(first + i * 384, 384), 384)
        dst[at, :] = wide[at, :].astype(jnp.bfloat16)
        return carry

    lax.fori_loop(0, rows // 384, step, 0)


def peer_at(group, i, sign):
    s, p = lax.axis_index("seq"), lax.axis_index("exp")
    along_x, along_y, across = i // 8, lax.rem(i // 2, 4), lax.rem(i, 2)
    along_z = lax.rem(group + 8 - along_x - along_y, 4)
    x = lax.rem(s // 2 + sign * along_x + 4, 4)
    y = lax.rem(p // 4 + sign * along_y + 4, 4)
    z = lax.rem(lax.rem(p, 4) + sign * along_z + 4, 4)
    return (2 * x + lax.rem(s + across, 2), 4 * y + z)


def place_of(expert):
    s, p = lax.axis_index("seq"), lax.axis_index("exp")
    to_s, to_p = expert // 16, expert % 16
    along_x = (to_s // 2 - s // 2 + 4) % 4
    along_y = (to_p // 4 - p // 4 + 4) % 4
    along_z = (to_p % 4 - p % 4 + 4) % 4
    across = (to_s + s) % 2
    return (along_x + along_y + along_z) % 4 * 32 + along_x * 8 + along_y * 2 + across


def exchange_start(group, sign, src, dst, send_sem, recv_sem, own_sem, chunk):
    members = src.shape[0] // chunk // GROUPS

    def step(i, carry):
        at = pl.ds(pl.multiple_of((group * members + i) * chunk, chunk), chunk)
        pltpu.make_async_remote_copy(
            src_ref=src.at[at],
            dst_ref=dst.at[at],
            send_sem=send_sem.at[group],
            recv_sem=recv_sem.at[group],
            device_id=peer_at(group, i, sign),
            device_id_type=MESH,
        ).start()
        return carry

    if group == 0:
        own = pl.ds(0, chunk)
        pltpu.make_async_copy(src.at[own], dst.at[own], own_sem).start()
    lax.fori_loop(1 if group == 0 else 0, members, step, 0)


def group_rows(group, src, chunk):
    members = src.shape[0] // chunk // GROUPS
    first = group * members + (1 if group == 0 else 0)
    return pl.ds(first * chunk, ((group + 1) * members - first) * chunk)


def exchange_wait(group, src, dst, recv_sem, own_sem, chunk):
    if group == 0:
        own = pl.ds(0, chunk)
        pltpu.make_async_copy(src.at[own], dst.at[own], own_sem).wait()
    at = group_rows(group, src, chunk)
    pltpu.make_async_copy(src.at[at], dst.at[at], recv_sem.at[group]).wait()


def exchange_sent(group, src, dst, send_sem, chunk):
    at = group_rows(group, src, chunk)
    pltpu.make_async_copy(src.at[at], dst.at[at], send_sem.at[group]).wait()


def experts_kernel(
    h_ref, row_ref, col_ref, encw_hbm, encb_ref, decw_hbm, decb_ref,
    picked_ref, grad_ref,
    encw, decw, wide, send, recv, back, ret, slot_rows, centered, latent, gated, residue,
    weight_sem, own_sem, send_sem, recv_sem, send_back_sem, recv_back_sem,
):
    tokens, width = h_ref.shape
    slots = slot_rows.shape[0]
    latents = latent.shape[1]
    lanes = width // TILE
    members = lax.axis_size("seq") * lax.axis_size("exp") // GROUPS
    chunk = slots // (members * GROUPS) * lanes
    part_slots = slots // GROUPS
    part_rows = part_slots * lanes
    barrier = pltpu.get_barrier_semaphore()

    for group in range(GROUPS):

        def greet(i, carry):
            pl.semaphore_signal(
                barrier, inc=1, device_id=peer_at(group, i, 1), device_id_type=MESH
            )
            return carry

        lax.fori_loop(1 if group == 0 else 0, members, greet, 0)
    enc_copy = pltpu.make_async_copy(encw_hbm, encw, weight_sem.at[0])
    dec_copy = pltpu.make_async_copy(decw_hbm, decw, weight_sem.at[1])
    enc_copy.start()
    dec_copy.start()

    for group in range(GROUPS):
        first = group * part_rows
        place = lax.broadcasted_iota(jnp.int32, (part_slots, tokens), 0) + group * part_slots
        pick = jnp.where(place == row_ref[...], 1.0, 0.0)
        free = (1.0 - jnp.sum(pick, axis=1, keepdims=True)) * EMPTY
        pick = pick.astype(jnp.bfloat16)
        for n in range(lanes // 2):
            rows = jnp.dot(
                pick,
                h_ref[:, 2 * n * TILE : 2 * (n + 1) * TILE],
                preferred_element_type=jnp.float32,
            )
            if n == 0:
                rows = rows + free
            wide[pl.ds(first + 2 * n, part_slots, stride=lanes), :] = rows[:, :TILE]
            wide[pl.ds(first + 2 * n + 1, part_slots, stride=lanes), :] = rows[:, TILE:]
        narrow(wide, send, first, part_rows)
        if group == 0:
            pl.semaphore_wait(barrier, members * GROUPS - 1)
        exchange_start(group, 1, send, recv, send_sem, recv_sem, own_sem.at[0], chunk)

    enc_copy.wait()
    dec_copy.wait()
    for group in range(GROUPS):
        first = group * part_rows
        mine = slice(group * part_slots, (group + 1) * part_slots)
        exchange_wait(group, send, recv, recv_sem, own_sem.at[0], chunk)
        widen(recv, wide, first, part_rows)
        live = wide[pl.ds(first, part_slots, stride=lanes), :][:, :1] < 0.5 * EMPTY
        for c in range(lanes):
            at = slice(c * TILE, (c + 1) * TILE)
            part = wide[pl.ds(first + c, part_slots, stride=lanes), :]
            if c < 2:
                part = jnp.where(live, part, 0.0)
            slot_rows[mine, at] = part.astype(jnp.bfloat16)
            centered[mine, at] = (part - decb_ref[:, at]).astype(jnp.bfloat16)
        for n in range(latents // 256):
            at = slice(n * 256, (n + 1) * 256)
            pre = jnp.dot(centered[mine, :], encw[:, at], preferred_element_type=jnp.float32)
            act = jnp.maximum(pre + encb_ref[:, at], 0.0)
            latent[mine, at] = act.astype(jnp.bfloat16)
            gated[mine, at] = jnp.where(live, act, 0.0).astype(jnp.bfloat16)
        for n in range(lanes // 2):
            at = slice(2 * n * TILE, 2 * (n + 1) * TILE)
            rebuilt = jnp.dot(latent[mine, :], decw[:, at], preferred_element_type=jnp.float32)
            rebuilt = (rebuilt + decb_ref[:, at]).astype(jnp.bfloat16).astype(jnp.float32)
            error = rebuilt - slot_rows[mine, at].astype(jnp.float32)
            residue[mine, at] = error.astype(jnp.bfloat16)
            wide[pl.ds(first + 2 * n, part_slots, stride=lanes), :] = rebuilt[:, :TILE]
            wide[pl.ds(first + 2 * n + 1, part_slots, stride=lanes), :] = rebuilt[:, TILE:]
        narrow(wide, back, first, part_rows)
        exchange_start(group, -1, back, ret, send_back_sem, recv_back_sem, own_sem.at[1], chunk)

    def grad_step(n, carry):
        at = pl.ds(pl.multiple_of(n * 256, 256), 256)
        grad_ref[at, :] = lax.dot_general(
            gated[:, at], residue[...], (((0,), (0,)), ((), ())),
            preferred_element_type=jnp.float32,
        ).astype(jnp.bfloat16)
        return carry

    lax.fori_loop(0, latents // 256, grad_step, 0)
    unplace = lax.broadcasted_iota(jnp.int32, (tokens, slots), 1) == col_ref[...]
    unpick = jnp.where(unplace, 1.0, 0.0).astype(jnp.bfloat16)

    for group in range(GROUPS):
        first = group * part_rows
        mine = slice(group * part_slots, (group + 1) * part_slots)
        exchange_wait(group, back, ret, recv_back_sem, own_sem.at[1], chunk)
        widen(ret, wide, first, part_rows)
        for c in range(lanes):
            slot_rows[mine, c * TILE : (c + 1) * TILE] = wide[
                pl.ds(first + c, part_slots, stride=lanes), :
            ].astype(jnp.bfloat16)
    for n in range(width // 256):
        at = slice(n * 256, (n + 1) * 256)
        picked_ref[:, at] = jnp.dot(
            unpick, slot_rows[:, at], preferred_element_type=jnp.float32
        ).astype(jnp.bfloat16)
    for group in range(GROUPS):
        exchange_sent(group, send, recv, send_sem, chunk)
        exchange_sent(group, back, ret, send_back_sem, chunk)


def run_experts(harvested, target, enc_weight, enc_bias, dec_weight, dec_bias, slots):
    tokens, width = harvested.shape
    latents = enc_bias.shape[0]
    lanes = width // TILE
    vmem = pl.BlockSpec(memory_space=pltpu.VMEM)
    hbm = pl.BlockSpec(memory_space=pl.ANY)
    tiles = pltpu.VMEM((slots * lanes, TILE), jnp.bfloat16)
    return pl.pallas_call(
        experts_kernel,
        out_shape=(
            jax.ShapeDtypeStruct((tokens, width), jnp.bfloat16),
            jax.ShapeDtypeStruct((latents, width), jnp.bfloat16),
        ),
        in_specs=[vmem, vmem, vmem, hbm, vmem, hbm, vmem],
        out_specs=(vmem, vmem),
        scratch_shapes=[
            pltpu.VMEM((width, latents), jnp.bfloat16),
            pltpu.VMEM((latents, width), jnp.bfloat16),
            pltpu.VMEM((slots * lanes, TILE), jnp.float32),
            tiles, tiles, tiles, tiles,
            pltpu.VMEM((slots, width), jnp.bfloat16),
            pltpu.VMEM((slots, width), jnp.bfloat16),
            pltpu.VMEM((slots, latents), jnp.bfloat16),
            pltpu.VMEM((slots, latents), jnp.bfloat16),
            pltpu.VMEM((slots, width), jnp.bfloat16),
            pltpu.SemaphoreType.DMA((2,)),
            pltpu.SemaphoreType.DMA((2,)),
            *[pltpu.SemaphoreType.DMA((GROUPS,))] * 4,
        ],
        compiler_params=pltpu.CompilerParams(
            collective_id=0, has_side_effects=True, vmem_limit_bytes=48 * 2**20
        ),
    )(
        harvested, target[None, :], target[:, None], enc_weight, enc_bias[None, :], dec_weight,
        dec_bias[None, :],
    )


def finish_kernel(h_ref, picked_ref, kept_ref, bias_ref, grad_ref,
                  h_out, recon_out, error_out, grad_out, recon, error, sem):
    grad_copy = pltpu.make_async_copy(grad_ref, grad_out, sem.at[0])
    h_copy = pltpu.make_async_copy(h_ref, h_out, sem.at[1])
    grad_copy.start()
    h_copy.start()
    blank = bias_ref[...].astype(jnp.bfloat16).astype(jnp.float32)
    value = jnp.where(kept_ref[...] >= 0, picked_ref[...].astype(jnp.float32), blank)
    recon[...] = value.astype(jnp.bfloat16)
    recon_copy = pltpu.make_async_copy(recon, recon_out, sem.at[2])
    recon_copy.start()
    error[...] = (value - h_ref[...].astype(jnp.float32)).astype(jnp.bfloat16)
    error_copy = pltpu.make_async_copy(error, error_out, sem.at[3])
    error_copy.start()
    for copy in (grad_copy, h_copy, recon_copy, error_copy):
        copy.wait()


def run_finish(harvested, picked, slot_ids, dec_bias, dec_grad):
    rows = jax.ShapeDtypeStruct(harvested.shape, jnp.bfloat16)
    vmem = pl.BlockSpec(memory_space=pltpu.VMEM)
    hbm = pl.BlockSpec(memory_space=pl.ANY)
    return pl.pallas_call(
        finish_kernel,
        out_shape=(rows, rows, rows, jax.ShapeDtypeStruct(dec_grad.shape, jnp.bfloat16)),
        in_specs=[vmem] * 4 + [hbm],
        out_specs=(hbm,) * 4,
        scratch_shapes=[
            pltpu.VMEM(harvested.shape, jnp.bfloat16),
            pltpu.VMEM(harvested.shape, jnp.bfloat16),
            pltpu.SemaphoreType.DMA((4,)),
        ],
        compiler_params=pltpu.CompilerParams(vmem_limit_bytes=16 * 2**20),
    )(harvested, picked, slot_ids[:, None], dec_bias[None, :], dec_grad)


def shards(
    query_rows,
    key_rows,
    value_matrix,
    doc_ids,
    out_weight,
    enc_weight,
    enc_bias,
    dec_weight,
    dec_bias,
    expert_ids,
    slot_ids,
):
    local_tokens = query_rows.shape[1]
    seq_groups = lax.axis_size("seq")
    exp_groups = lax.axis_size("exp")
    devices_all = seq_groups * exp_groups
    doc_row = doc_ids[0]
    doc_mine = lax.dynamic_slice_in_dim(
        doc_row, lax.axis_index("seq") * local_tokens, local_tokens
    )
    harvested = run_attention(
        query_rows[0], key_rows[0], value_matrix[0], doc_mine, doc_row, out_weight, seq_groups
    )
    local_experts = enc_weight.shape[0]
    experts_all = local_experts * devices_all
    capacity = 2 * local_tokens // experts_all
    expert_here = expert_ids[0]
    slot_here = slot_ids[0]
    kept_token = slot_here >= 0
    slot_count = experts_all * capacity
    target = jnp.where(kept_token, place_of(expert_here) * capacity + slot_here, slot_count)
    picked_rows, dec_grad = run_experts(
        harvested, target, enc_weight[0], enc_bias[0], dec_weight[0], dec_bias, slot_count
    )
    harvested, reconstruction, error_rows, dec_grad = run_finish(
        harvested, picked_rows, slot_here, dec_bias, dec_grad
    )
    return (harvested[None], reconstruction[None], error_rows[None], dec_grad[None])


def solution(mesh):
    return jax.shard_map(
        shards,
        mesh=mesh,
        in_specs=(
            P("exp", "seq", None),
            P("exp", "seq", None),
            P("exp", "seq", None),
            P("exp", None),
            P(("seq", "exp"), None),
            P(("seq", "exp"), None, None),
            P(("seq", "exp"), None),
            P(("seq", "exp"), None, None),
            P(),
            P("exp", "seq"),
            P("exp", "seq"),
        ),
        out_specs=(
            P("exp", "seq", None),
            P("exp", "seq", None),
            P("exp", "seq", None),
            P(("seq", "exp"), None, None),
        ),
        check_vma=False,
    )
```

```python
import math

import jax
import jax.numpy as jnp
from jax import lax
from jax.experimental import pallas as pl
from jax.experimental.pallas import tpu as pltpu
from jax.sharding import PartitionSpec as P

HEAD_DIMENSION = 128
MESH = pl.DeviceIdType.MESH
TILE = 128
EMPTY = 1e30
PARTS = ((0, 384), (384, 256), (640, 384))
ORDERS = ("xyz", "yzx", "xzy")


def attention_part(
    q_hbm, k_hbm, v_hbm, doc_hbm, w_hbm,
    out_ref,
    doc_row, queries, kv, w_a, w_b, w_c, attended, bias, result, half_in,
    send_sem, recv_sem, local_sem,
):
    s, p = lax.axis_index("seq"), lax.axis_index("exp")
    place = {"x": s // 2, "y": p // 4, "z": lax.rem(p, 4)}
    core = lax.rem(s, 2)
    tokens = queries.shape[0]
    kv_width = k_hbm.shape[1]
    span = kv.shape[0] * tokens
    half = out_ref.shape[1] // 2
    heads = queries.shape[1] // HEAD_DIMENSION
    group = heads // (kv_width // HEAD_DIMENSION)
    scale = math.log2(math.e) / math.sqrt(HEAD_DIMENSION)
    parts = (w_a, w_b, w_c)
    partner = (2 * place["x"] + 1 - core, p)

    def beside(axis, step):
        at = dict(place)
        at[axis] = lax.rem(at[axis] + step + 4, 4)
        return (2 * at["x"] + core, 4 * at["y"] + at["z"])

    peers = [partner] + [beside(axis, step) for axis in "xyz" for step in (1, -1)]
    barrier = pltpu.get_barrier_semaphore()
    for peer in peers:
        pl.semaphore_signal(barrier, inc=1, device_id=peer, device_id_type=MESH)

    started = []

    def send(src, dst, peer):
        copy = pltpu.make_async_remote_copy(
            src_ref=src,
            dst_ref=dst,
            send_sem=send_sem.at[len(started)],
            recv_sem=recv_sem.at[len(started)],
            device_id=peer,
            device_id_type=MESH,
        )
        started.append(copy)
        copy.start()
        return copy

    def arrive(copies):
        for copy in copies:
            copy.wait_recv()

    own = [
        (k_hbm, kv.at[s, :, pl.ds(0, kv_width)]),
        (v_hbm, kv.at[s, :, pl.ds(kv_width, kv_width)]),
    ]
    for (first, wide), buffer in zip(PARTS, parts):
        columns = pl.ds(pl.multiple_of(core * half + first, TILE), wide)
        own.append((w_hbm.at[:, columns], buffer.at[place["x"], core, place["y"], place["z"]]))
    own.append((doc_hbm, doc_row))
    own.append((q_hbm, queries))
    own = [pltpu.make_async_copy(a, b, local_sem.at[i]) for i, (a, b) in enumerate(own)]
    for copy in own:
        copy.start()
    own[0].wait()
    own[1].wait()
    pl.semaphore_wait(barrier, len(peers))

    kv_near = [send(kv.at[s], kv.at[s], beside("x", step)) for step in (1, -1)]
    kv_own_pair = send(kv.at[s], kv.at[s], partner)
    w_pair = []
    for (first, wide), buffer in zip(PARTS, parts):
        columns = pl.ds(pl.multiple_of((1 - core) * half + first, TILE), wide)
        w_pair.append(
            send(
                w_hbm.at[:, columns],
                buffer.at[place["x"], core, place["y"], place["z"]],
                partner,
            )
        )

    def view(part, offsets, row=None):
        at = {}
        for axis, offset in zip(ORDERS[part], offsets):
            if offset is None:
                at[axis] = pl.ds(0, 4)
            else:
                at[axis] = pl.ds(lax.rem(place[axis] + offset + 4, 4), 1)
        rows = pl.ds(0, 2) if row is None else pl.ds(row, 1)
        return parts[part].at[at["x"], rows, at["y"], at["z"]]

    def near(stage, offsets):
        copies = []
        for part in range(3):
            block = view(part, offsets)
            for step in (1, -1):
                copies.append(send(block, block, beside(ORDERS[part][stage], step)))
        return copies

    def far(stage, offsets):
        copies = []
        for part in range(3):
            for step, row in ((1, 0), (-1, 1)):
                at = offsets[:stage] + (-step,) + offsets[stage + 1 :]
                block = view(part, at, row)
                copies.append(send(block, block, beside(ORDERS[part][stage], step)))
        return copies

    def attend(first, last, blocks):
        keys = blocks * tokens

        def one_head(h, carry):
            g = h // group
            q_at = pl.ds(pl.multiple_of(h * HEAD_DIMENSION, HEAD_DIMENSION), HEAD_DIMENSION)
            k_at = pl.ds(pl.multiple_of(g * HEAD_DIMENSION, HEAD_DIMENSION), HEAD_DIMENSION)
            v_at = pl.ds(
                pl.multiple_of(kv_width + g * HEAD_DIMENSION, HEAD_DIMENSION), HEAD_DIMENSION
            )
            key_part = kv[:blocks, :, k_at].reshape(keys, HEAD_DIMENSION)
            value_part = kv[:blocks, :, v_at].reshape(keys, HEAD_DIMENSION)
            scores = lax.dot_general(
                queries[:, q_at], key_part, (((1,), (1,)), ((), ())),
                preferred_element_type=jnp.float32,
            )
            scores = scores + bias[:, :keys]
            highest = jnp.max(scores, axis=1, keepdims=True)
            weights = jnp.exp2((scores - highest) * scale)
            total = jnp.sum(weights, axis=1, keepdims=True)
            mixed = jnp.dot(
                weights.astype(jnp.bfloat16), value_part, preferred_element_type=jnp.float32
            )
            attended[core, :, q_at] = (mixed / total).astype(jnp.bfloat16)
            return carry

        lax.fori_loop(first, last, one_head, 0)

    def attend_some(quarter):
        first, last = quarter * heads // 4, (quarter + 1) * heads // 4
        for chips in range(1, 5):

            @pl.when(place["x"] == chips - 1)
            def _():
                attend(first, last, 2 * chips)

        columns = pl.ds(first * HEAD_DIMENSION, (last - first) * HEAD_DIMENSION)
        piece = attended.at[core, :, columns]
        return send(piece, piece, partner)

    arrive(w_pair)
    for copy in own[2:5]:
        copy.wait()
    near_1 = near(0, (0, 0, 0))
    near_2 = near(1, (0, 0, 0))
    near_3 = near(2, (0, 0, 0))
    own[5].wait()
    rows_at = s * tokens + lax.broadcasted_iota(jnp.int32, (tokens, span), 0)
    keys_at = lax.broadcasted_iota(jnp.int32, (tokens, span), 1)
    doc_all = doc_row[...].astype(jnp.float32)
    doc_mine = jnp.sum(jnp.where(rows_at == keys_at, doc_all, 0.0), axis=1, keepdims=True)
    visible = (rows_at >= keys_at) & (doc_mine == doc_all)
    bias[...] = jnp.where(visible, 0.0, -EMPTY)
    own[6].wait()
    arrive([kv_own_pair])
    arrive(near_1)
    far_1 = far(0, (None, 0, 0))
    for offset in (-1, 1):
        near_2 += near(1, (offset, 0, 0))
        near_3 += near(2, (offset, 0, 0))
    arrive(far_1)
    near_2 += near(1, (2, 0, 0))
    near_3 += near(2, (2, 0, 0))
    arrive(kv_near)
    kv_far = []
    for step, first in ((1, 0), (-1, tokens // 2)):
        origin = 2 * lax.rem(place["x"] - step + 4, 4) + core
        piece = kv.at[origin, pl.ds(first, tokens // 2)]
        kv_far.append(send(piece, piece, beside("x", step)))
    kv_pair = []
    for step in (1, -1):
        piece = kv.at[2 * lax.rem(place["x"] - step + 4, 4) + core]
        kv_pair.append(send(piece, piece, partner))
    arrive(near_2)
    far_2 = far(1, (None, None, 0))
    near_3b = near(2, (None, -1, 0)) + near(2, (None, 1, 0))
    arrive(kv_far)
    piece = kv.at[2 * lax.rem(place["x"] + 2, 4) + core]
    kv_pair.append(send(piece, piece, partner))
    arrive(far_2)
    near_3c = near(2, (None, 2, 0))
    arrive(kv_pair)
    across = [attend_some(0)]
    arrive(near_3)
    far_3 = far(2, (None, 0, None))
    across.append(attend_some(1))
    arrive(near_3b)
    far_3 += far(2, (None, -1, None)) + far(2, (None, 1, None))
    across.append(attend_some(2))
    arrive(near_3c)
    far_3 += far(2, (None, 2, None))
    across.append(attend_some(3))
    arrive(across)
    arrive(far_3)

    rows = attended.shape[1] * 2
    for (first, wide), buffer in zip(PARTS, parts):
        both = jnp.dot(
            attended[...].reshape(rows, heads * HEAD_DIMENSION),
            buffer[...].reshape(heads * HEAD_DIMENSION, wide),
            preferred_element_type=jnp.float32,
        )
        result[:, :, first : first + wide] = both.astype(jnp.bfloat16).reshape(2, tokens, wide)
    back = send(result.at[1 - core], half_in, partner)
    out_ref[:, pl.ds(pl.multiple_of(core * half, half), half)] = result[core]
    arrive([back])
    out_ref[:, pl.ds(pl.multiple_of((1 - core) * half, half), half)] = half_in[...]
    for copy in started:
        copy.wait_send()


GROUPS = 2
VMEM_MIB = 60


def widen(src, wide, first, rows):
    def step(i, carry):
        at = pl.ds(pl.multiple_of(first + i * 384, 384), 384)
        wide[at, :] = src[at, :].astype(jnp.float32)
        return carry

    lax.fori_loop(0, rows // 384, step, 0)


def narrow(wide, dst, first, rows):
    def step(i, carry):
        at = pl.ds(pl.multiple_of(first + i * 384, 384), 384)
        dst[at, :] = wide[at, :].astype(jnp.bfloat16)
        return carry

    lax.fori_loop(0, rows // 384, step, 0)


def peer_at(group, i, sign):
    s, p = lax.axis_index("seq"), lax.axis_index("exp")
    i = i + group * (lax.axis_size("seq") * lax.axis_size("exp") // GROUPS)
    turn, i = i // 32, lax.rem(i, 32)
    along_x, along_y, across = i // 8, lax.rem(i // 2, 4), lax.rem(i, 2)
    along_z = lax.rem(turn + 8 - along_x - along_y, 4)
    x = lax.rem(s // 2 + sign * along_x + 4, 4)
    y = lax.rem(p // 4 + sign * along_y + 4, 4)
    z = lax.rem(lax.rem(p, 4) + sign * along_z + 4, 4)
    return (2 * x + lax.rem(s + across, 2), 4 * y + z)


def place_of(expert):
    s, p = lax.axis_index("seq"), lax.axis_index("exp")
    to_s, to_p = expert >> 4, expert & 15
    along_x = ((to_s >> 1) - s // 2) & 3
    along_y = ((to_p >> 2) - p // 4) & 3
    along_z = (to_p - p) & 3
    across = (to_s + s) & 1
    turn = (along_x + along_y + along_z) & 3
    return turn * 32 + along_x * 8 + along_y * 2 + across


def exchange_start(group, sign, src, dst, send_sem, recv_sem, own_sem, chunk):
    members = src.shape[0] // chunk // GROUPS

    def step(i, carry):
        at = pl.ds(pl.multiple_of((group * members + i) * chunk, chunk), chunk)
        pltpu.make_async_remote_copy(
            src_ref=src.at[at],
            dst_ref=dst.at[at],
            send_sem=send_sem.at[group],
            recv_sem=recv_sem.at[group],
            device_id=peer_at(group, i, sign),
            device_id_type=MESH,
        ).start()
        return carry

    if group == 0:
        own = pl.ds(0, chunk)
        pltpu.make_async_copy(src.at[own], dst.at[own], own_sem).start()
    lax.fori_loop(1 if group == 0 else 0, members, step, 0)


def group_rows(group, src, chunk):
    members = src.shape[0] // chunk // GROUPS
    first = group * members + (1 if group == 0 else 0)
    return pl.ds(first * chunk, ((group + 1) * members - first) * chunk)


def exchange_wait(group, src, dst, recv_sem, own_sem, chunk):
    if group == 0:
        own = pl.ds(0, chunk)
        pltpu.make_async_copy(src.at[own], dst.at[own], own_sem).wait()
    at = group_rows(group, src, chunk)
    pltpu.make_async_copy(src.at[at], dst.at[at], recv_sem.at[group]).wait()


def exchange_sent(group, src, dst, send_sem, chunk):
    at = group_rows(group, src, chunk)
    pltpu.make_async_copy(src.at[at], dst.at[at], send_sem.at[group]).wait()


def experts_load(hbm, vmem, sem):
    copies = [pltpu.make_async_copy(a, b, sem.at[i]) for i, (a, b) in enumerate(zip(hbm, vmem))]
    for copy in copies:
        copy.start()
    return copies


def experts_part(
    loads, h_ref, recon_out, error_out, grad_out, out_sem,
    encw, decw, expert_row, slot_row, encb_ref, decb_ref, picks,
    wide, send, recv, back, ret, slot_rows, centered, latent, gated, residue,
    own_sem, send_sem, recv_sem, send_back_sem, recv_back_sem,
):
    tokens, width = h_ref.shape
    slots = slot_rows.shape[0]
    latents = latent.shape[1]
    lanes = width // TILE
    members = lax.axis_size("seq") * lax.axis_size("exp") // GROUPS
    chunk = slots // (members * GROUPS) * lanes
    part_slots = slots // GROUPS
    part_rows = part_slots * lanes
    enc_copy, dec_copy, *small = loads
    for copy in small:
        copy.wait()
    capacity = slots // (members * GROUPS)
    target = jnp.where(
        slot_row[...] >= 0, place_of(expert_row[...]) * capacity + slot_row[...], slots
    )

    for group in range(GROUPS):
        first = group * part_rows
        place = lax.broadcasted_iota(jnp.int32, (part_slots, tokens), 0) + group * part_slots
        pick = jnp.where(place == target, 1.0, 0.0)
        free = (1.0 - jnp.sum(pick, axis=1, keepdims=True)) * EMPTY
        pick = pick.astype(jnp.bfloat16)
        picks[group * part_slots : (group + 1) * part_slots, :] = pick
        for n in range(lanes // 2):
            rows = jnp.dot(
                pick,
                h_ref[:, 2 * n * TILE : 2 * (n + 1) * TILE],
                preferred_element_type=jnp.float32,
            )
            if n == 0:
                rows = rows + free
            wide[pl.ds(first + 2 * n, part_slots, stride=lanes), :] = rows[:, :TILE]
            wide[pl.ds(first + 2 * n + 1, part_slots, stride=lanes), :] = rows[:, TILE:]
        narrow(wide, send, first, part_rows)
        exchange_start(group, 1, send, recv, send_sem, recv_sem, own_sem.at[0], chunk)

    enc_copy.wait()
    dec_copy.wait()
    for group in range(GROUPS):
        first = group * part_rows
        mine = slice(group * part_slots, (group + 1) * part_slots)
        exchange_wait(group, send, recv, recv_sem, own_sem.at[0], chunk)
        widen(recv, wide, first, part_rows)
        live = wide[pl.ds(first, part_slots, stride=lanes), :][:, :1] < 0.5 * EMPTY
        for c in range(lanes):
            at = slice(c * TILE, (c + 1) * TILE)
            part = wide[pl.ds(first + c, part_slots, stride=lanes), :]
            if c < 2:
                part = jnp.where(live, part, 0.0)
            slot_rows[mine, at] = part.astype(jnp.bfloat16)
            centered[mine, at] = (part - decb_ref[:, at]).astype(jnp.bfloat16)
        for n in range(latents // 256):
            at = slice(n * 256, (n + 1) * 256)
            pre = jnp.dot(centered[mine, :], encw[:, at], preferred_element_type=jnp.float32)
            act = jnp.maximum(pre + encb_ref[:, at], 0.0)
            latent[mine, at] = act.astype(jnp.bfloat16)
            gated[mine, at] = jnp.where(live, act, 0.0).astype(jnp.bfloat16)
        for n in range(lanes // 2):
            at = slice(2 * n * TILE, 2 * (n + 1) * TILE)
            rebuilt = jnp.dot(latent[mine, :], decw[:, at], preferred_element_type=jnp.float32)
            rebuilt = (rebuilt + decb_ref[:, at]).astype(jnp.bfloat16).astype(jnp.float32)
            error = rebuilt - slot_rows[mine, at].astype(jnp.float32)
            residue[mine, at] = error.astype(jnp.bfloat16)
            wide[pl.ds(first + 2 * n, part_slots, stride=lanes), :] = rebuilt[:, :TILE]
            wide[pl.ds(first + 2 * n + 1, part_slots, stride=lanes), :] = rebuilt[:, TILE:]
        narrow(wide, back, first, part_rows)
        exchange_start(group, -1, back, ret, send_back_sem, recv_back_sem, own_sem.at[1], chunk)

    outs = []
    for n in range(latents // 256):
        at = slice(n * 256, (n + 1) * 256)
        decw[at, :] = lax.dot_general(
            gated[:, at], residue[...], (((0,), (0,)), ((), ())),
            preferred_element_type=jnp.float32,
        ).astype(jnp.bfloat16)
        rows = pl.ds(n * 256, 256)
        outs.append(pltpu.make_async_copy(decw.at[rows], grad_out.at[rows], out_sem.at[3 + n]))
        outs[-1].start()

    def gather_back(rows):
        return lax.dot_general(
            picks[...], rows, (((0,), (0,)), ((), ())), preferred_element_type=jnp.float32
        )

    kept = gather_back(jnp.ones((slots, TILE), jnp.bfloat16))[:, :1] > 0.5
    for group in range(GROUPS):
        first = group * part_rows
        mine = slice(group * part_slots, (group + 1) * part_slots)
        exchange_wait(group, back, ret, recv_back_sem, own_sem.at[1], chunk)
        widen(ret, wide, first, part_rows)
        for c in range(lanes):
            slot_rows[mine, c * TILE : (c + 1) * TILE] = wide[
                pl.ds(first + c, part_slots, stride=lanes), :
            ].astype(jnp.bfloat16)
    for n in range(width // 256):
        at = slice(n * 256, (n + 1) * 256)
        rows = jnp.where(kept, gather_back(slot_rows[:, at]), decb_ref[:, at]).astype(jnp.bfloat16)
        centered[:tokens, at] = rows
        error = rows.astype(jnp.float32) - h_ref[:, at].astype(jnp.float32)
        centered[tokens : 2 * tokens, at] = error.astype(jnp.bfloat16)
    for i, out in enumerate((recon_out, error_out)):
        rows = centered.at[pl.ds(i * tokens, tokens)]
        outs.append(pltpu.make_async_copy(rows, out, out_sem.at[1 + i]))
        outs[-1].start()
    for copy in outs:
        copy.wait()
    for group in range(GROUPS):
        exchange_sent(group, send, recv, send_sem, chunk)
        exchange_sent(group, back, ret, send_back_sem, chunk)


def whole_kernel(
    q_hbm, k_hbm, v_hbm, doc_hbm, w_hbm,
    expert_hbm, slot_hbm, encw_hbm, encb_hbm, decw_hbm, decb_hbm,
    h_out, recon_out, error_out, grad_out, *scratch,
):
    first, second = scratch[:13], scratch[13:-3]
    load_sem, out_sem, h_ref = scratch[-3:]
    loads = experts_load(
        (encw_hbm, decw_hbm, expert_hbm, slot_hbm, encb_hbm, decb_hbm), second[:6], load_sem
    )
    attention_part(q_hbm, k_hbm, v_hbm, doc_hbm, w_hbm, h_ref, *first)
    h_copy = pltpu.make_async_copy(h_ref, h_out, out_sem.at[0])
    h_copy.start()
    experts_part(loads, h_ref, recon_out, error_out, grad_out, out_sem, *second)
    h_copy.wait()


def run_whole(
    query, key, value, doc_all, out_weight, experts, slot_ids, enc_weight, enc_bias, dec_weight,
    dec_bias, seq_groups, slots,
):
    tokens, q_width = query.shape
    kv_width = key.shape[1]
    span = tokens * seq_groups
    rows, width = out_weight.shape
    latents = enc_bias.shape[1]
    lanes = width // TILE
    hbm = pl.BlockSpec(memory_space=pl.ANY)
    dma = pltpu.SemaphoreType.DMA
    copies = 128

    def half(*shape):
        return pltpu.VMEM(shape, jnp.bfloat16)

    def full(*shape):
        return pltpu.VMEM(shape, jnp.float32)

    return pl.pallas_call(
        whole_kernel,
        out_shape=(
            *[jax.ShapeDtypeStruct((tokens, width), jnp.bfloat16)] * 3,
            jax.ShapeDtypeStruct((latents, width), jnp.bfloat16),
        ),
        in_specs=[hbm] * 11,
        out_specs=(hbm,) * 4,
        scratch_shapes=[
            pltpu.VMEM((1, span), jnp.int32),
            half(tokens, q_width),
            half(seq_groups, tokens, 2 * kv_width),
            *[half(4, 2, 4, 4, rows, wide) for _, wide in PARTS],
            half(2, tokens, q_width),
            full(tokens, span),
            half(2, tokens, width // 2),
            half(tokens, width // 2),
            dma((copies,)),
            dma((copies,)),
            dma((7,)),
            half(width, latents),
            half(latents, width),
            pltpu.VMEM((1, tokens), jnp.int32),
            pltpu.VMEM((1, tokens), jnp.int32),
            full(1, latents),
            full(1, width),
            half(slots, tokens),
            full(slots * lanes, TILE),
            *[half(slots * lanes, TILE)] * 4,
            half(slots, width),
            half(slots, width),
            half(slots, latents),
            half(slots, latents),
            half(slots, width),
            dma((2,)),
            *[dma((GROUPS,))] * 4,
            dma((6,)),
            dma((3 + latents // 256,)),
            half(tokens, width),
        ],
        compiler_params=pltpu.CompilerParams(
            collective_id=0, has_side_effects=True, vmem_limit_bytes=VMEM_MIB * 2**20
        ),
    )(
        query, key, value, doc_all, out_weight, experts, slot_ids, enc_weight, enc_bias,
        dec_weight, dec_bias[None, :],
    )


def finish_kernel(*refs):
    sources, targets, held, sems = refs[:4], refs[4:8], refs[8:12], refs[12:]
    pairs = []
    for source, hold, target in zip(sources, held, targets):
        rows = source.shape[0]
        for first in range(0, rows, 192):
            at = pl.ds(first, min(192, rows - first))
            i = len(pairs)
            pairs.append(
                (
                    pltpu.make_async_copy(source.at[at], hold.at[at], sems[0].at[i]),
                    pltpu.make_async_copy(hold.at[at], target.at[at], sems[1].at[i]),
                )
            )
            pairs[-1][0].start()
    for fetch, store in pairs:
        fetch.wait()
        store.start()
    for fetch, store in pairs:
        store.wait()


def run_finish(*arrays):
    hbm = pl.BlockSpec(memory_space=pl.ANY)
    return pl.pallas_call(
        finish_kernel,
        out_shape=tuple(jax.ShapeDtypeStruct(a.shape, a.dtype) for a in arrays),
        in_specs=[hbm] * 4,
        out_specs=(hbm,) * 4,
        scratch_shapes=[
            *[pltpu.VMEM(a.shape, a.dtype) for a in arrays],
            pltpu.SemaphoreType.DMA((16,)),
            pltpu.SemaphoreType.DMA((16,)),
        ],
        compiler_params=pltpu.CompilerParams(vmem_limit_bytes=VMEM_MIB * 2**20),
    )(*arrays)


def shards(
    query_rows,
    key_rows,
    value_matrix,
    doc_ids,
    out_weight,
    enc_weight,
    enc_bias,
    dec_weight,
    dec_bias,
    expert_ids,
    slot_ids,
):
    local_tokens = query_rows.shape[1]
    seq_groups = lax.axis_size("seq")
    experts_all = enc_weight.shape[0] * seq_groups * lax.axis_size("exp")
    slot_count = 2 * local_tokens // experts_all * experts_all
    outputs = run_whole(
        query_rows[0], key_rows[0], value_matrix[0], doc_ids, out_weight, expert_ids, slot_ids,
        enc_weight[0], enc_bias, dec_weight[0], dec_bias, seq_groups, slot_count,
    )
    harvested, reconstruction, error_rows, dec_grad = run_finish(*outputs)
    return (harvested[None], reconstruction[None], error_rows[None], dec_grad[None])


def solution(mesh):
    return jax.shard_map(
        shards,
        mesh=mesh,
        in_specs=(
            P("exp", "seq", None),
            P("exp", "seq", None),
            P("exp", "seq", None),
            P("exp", None),
            P(("seq", "exp"), None),
            P(("seq", "exp"), None, None),
            P(("seq", "exp"), None),
            P(("seq", "exp"), None, None),
            P(),
            P("exp", "seq"),
            P("exp", "seq"),
        ),
        out_specs=(
            P("exp", "seq", None),
            P("exp", "seq", None),
            P("exp", "seq", None),
            P(("seq", "exp"), None, None),
        ),
        check_vma=False,
    )
```

```python
import math

import jax
import jax.numpy as jnp
from jax import lax
from jax.experimental import pallas as pl
from jax.experimental.pallas import tpu as pltpu
from jax.sharding import PartitionSpec as P

HEAD_DIMENSION = 128
MESH = pl.DeviceIdType.MESH
TILE = 128
EMPTY = 1e30
PARTS = ((0, 384), (384, 256), (640, 384))
ORDERS = ("xyz", "yzx", "xzy")


def attention_part(
    q_hbm, k_hbm, v_hbm, doc_hbm, w_hbm,
    out_ref,
    doc_row, queries, kv, w_a, w_b, w_c, attended, bias, result, half_in,
    send_sem, recv_sem, local_sem,
):
    s, p = lax.axis_index("seq"), lax.axis_index("exp")
    place = {"x": s // 2, "y": p // 4, "z": lax.rem(p, 4)}
    core = lax.rem(s, 2)
    tokens = queries.shape[0]
    kv_width = k_hbm.shape[1]
    span = kv.shape[0] * tokens
    half = out_ref.shape[1] // 2
    heads = queries.shape[1] // HEAD_DIMENSION
    group = heads // (kv_width // HEAD_DIMENSION)
    scale = math.log2(math.e) / math.sqrt(HEAD_DIMENSION)
    parts = (w_a, w_b, w_c)
    partner = (2 * place["x"] + 1 - core, p)

    def beside(axis, step):
        at = dict(place)
        at[axis] = lax.rem(at[axis] + step + 4, 4)
        return (2 * at["x"] + core, 4 * at["y"] + at["z"])

    peers = [partner] + [beside(axis, step) for axis in "xyz" for step in (1, -1)]
    barrier = pltpu.get_barrier_semaphore()
    for peer in peers:
        pl.semaphore_signal(barrier, inc=1, device_id=peer, device_id_type=MESH)

    started = []

    def send(src, dst, peer):
        copy = pltpu.make_async_remote_copy(
            src_ref=src,
            dst_ref=dst,
            send_sem=send_sem.at[len(started)],
            recv_sem=recv_sem.at[len(started)],
            device_id=peer,
            device_id_type=MESH,
        )
        started.append(copy)
        copy.start()
        return copy

    def arrive(copies):
        for copy in copies:
            copy.wait_recv()

    own = [
        (k_hbm, kv.at[s, :, pl.ds(0, kv_width)]),
        (v_hbm, kv.at[s, :, pl.ds(kv_width, kv_width)]),
    ]
    for (first, wide), buffer in zip(PARTS, parts):
        columns = pl.ds(pl.multiple_of(core * half + first, TILE), wide)
        own.append((w_hbm.at[:, columns], buffer.at[place["x"], core, place["y"], place["z"]]))
    own.append((doc_hbm, doc_row))
    own.append((q_hbm, queries))
    own = [pltpu.make_async_copy(a, b, local_sem.at[i]) for i, (a, b) in enumerate(own)]
    for copy in own:
        copy.start()
    own[0].wait()
    own[1].wait()
    pl.semaphore_wait(barrier, len(peers))

    w_pair = []
    for (first, wide), buffer in zip(PARTS, parts):
        columns = pl.ds(pl.multiple_of((1 - core) * half + first, TILE), wide)
        w_pair.append(
            send(
                w_hbm.at[:, columns],
                buffer.at[place["x"], core, place["y"], place["z"]],
                partner,
            )
        )

    def view(part, offsets, row=None):
        at = {}
        for axis, offset in zip(ORDERS[part], offsets):
            if offset is None:
                at[axis] = pl.ds(0, 4)
            else:
                at[axis] = pl.ds(lax.rem(place[axis] + offset + 4, 4), 1)
        rows = pl.ds(0, 2) if row is None else pl.ds(row, 1)
        return parts[part].at[at["x"], rows, at["y"], at["z"]]

    def near(stage, offsets):
        copies = []
        for part in range(3):
            block = view(part, offsets)
            for step in (1, -1):
                copies.append(send(block, block, beside(ORDERS[part][stage], step)))
        return copies

    def far(stage, offsets):
        copies = []
        for part in range(3):
            for step, row in ((1, 0), (-1, 1)):
                at = offsets[:stage] + (-step,) + offsets[stage + 1 :]
                block = view(part, at, row)
                copies.append(send(block, block, beside(ORDERS[part][stage], step)))
        return copies

    def attend(first, last, blocks):
        keys = blocks * tokens

        def one_head(h, carry):
            g = h // group
            q_at = pl.ds(pl.multiple_of(h * HEAD_DIMENSION, HEAD_DIMENSION), HEAD_DIMENSION)
            k_at = pl.ds(pl.multiple_of(g * HEAD_DIMENSION, HEAD_DIMENSION), HEAD_DIMENSION)
            v_at = pl.ds(
                pl.multiple_of(kv_width + g * HEAD_DIMENSION, HEAD_DIMENSION), HEAD_DIMENSION
            )
            key_part = kv[:blocks, :, k_at].reshape(keys, HEAD_DIMENSION)
            value_part = kv[:blocks, :, v_at].reshape(keys, HEAD_DIMENSION)
            scores = lax.dot_general(
                queries[:, q_at], key_part, (((1,), (1,)), ((), ())),
                preferred_element_type=jnp.float32,
            )
            scores = scores + bias[:, :keys]
            highest = jnp.max(scores, axis=1, keepdims=True)
            weights = jnp.exp2((scores - highest) * scale)
            total = jnp.sum(weights, axis=1, keepdims=True)
            mixed = jnp.dot(
                weights.astype(jnp.bfloat16), value_part, preferred_element_type=jnp.float32
            )
            attended[core, :, q_at] = (mixed / total).astype(jnp.bfloat16)
            return carry

        def four(i, carry):
            for j in range(4):
                one_head(4 * i + j, carry)
            return carry

        lax.fori_loop(first // 4, last // 4, four, 0)

    def attend_some(quarter):
        first, last = quarter * heads // 4, (quarter + 1) * heads // 4
        for chips in range(1, 5):

            @pl.when(place["x"] == chips - 1)
            def _():
                attend(first, last, 2 * chips)

        columns = pl.ds(first * HEAD_DIMENSION, (last - first) * HEAD_DIMENSION)
        piece = attended.at[core, :, columns]
        return send(piece, piece, partner)

    arrive(w_pair)
    for copy in own[2:5]:
        copy.wait()
    near_1 = near(0, (0, 0, 0))
    kv_near = [send(kv.at[s], kv.at[s], beside("x", step)) for step in (1, -1)]
    kv_own_pair = send(kv.at[s], kv.at[s], partner)
    near_2 = near(1, (0, 0, 0))
    near_3 = near(2, (0, 0, 0))
    own[5].wait()
    rows_at = s * tokens + lax.broadcasted_iota(jnp.int32, (tokens, span), 0)
    keys_at = lax.broadcasted_iota(jnp.int32, (tokens, span), 1)
    doc_all = doc_row[...].astype(jnp.float32)
    doc_mine = jnp.sum(jnp.where(rows_at == keys_at, doc_all, 0.0), axis=1, keepdims=True)
    visible = (rows_at >= keys_at) & (doc_mine == doc_all)
    bias[...] = jnp.where(visible, 0.0, -EMPTY)
    own[6].wait()
    arrive([kv_own_pair])
    arrive(near_1)
    far_1 = far(0, (None, 0, 0))
    for offset in (-1, 1):
        near_2 += near(1, (offset, 0, 0))
        near_3 += near(2, (offset, 0, 0))
    arrive(far_1)
    near_2 += near(1, (2, 0, 0))
    near_3 += near(2, (2, 0, 0))
    arrive(kv_near)
    kv_far = []
    for step, first in ((1, 0), (-1, tokens // 2)):
        origin = 2 * lax.rem(place["x"] - step + 4, 4) + core
        piece = kv.at[origin, pl.ds(first, tokens // 2)]
        kv_far.append(send(piece, piece, beside("x", step)))
    kv_pair = []
    for step in (1, -1):
        piece = kv.at[2 * lax.rem(place["x"] - step + 4, 4) + core]
        kv_pair.append(send(piece, piece, partner))
    arrive(near_2)
    far_2 = far(1, (None, None, 0))
    near_3b = near(2, (None, -1, 0)) + near(2, (None, 1, 0))
    arrive(kv_far)
    piece = kv.at[2 * lax.rem(place["x"] + 2, 4) + core]
    kv_pair.append(send(piece, piece, partner))
    arrive(far_2)
    near_3c = near(2, (None, 2, 0))
    arrive(kv_pair)
    across = [attend_some(0)]
    arrive(near_3)
    far_3 = far(2, (None, 0, None))
    across.append(attend_some(1))
    arrive(near_3b)
    far_3 += far(2, (None, -1, None)) + far(2, (None, 1, None))
    across.append(attend_some(2))
    arrive(near_3c)
    far_3 += far(2, (None, 2, None))
    across.append(attend_some(3))
    arrive(across)
    arrive(far_3)

    rows = attended.shape[1] * 2
    for (first, wide), buffer in zip(PARTS, parts):
        both = jnp.dot(
            attended[...].reshape(rows, heads * HEAD_DIMENSION),
            buffer[...].reshape(heads * HEAD_DIMENSION, wide),
            preferred_element_type=jnp.float32,
        )
        result[:, :, first : first + wide] = both.astype(jnp.bfloat16).reshape(2, tokens, wide)
    back = send(result.at[1 - core], half_in, partner)
    out_ref[:, pl.ds(pl.multiple_of(core * half, half), half)] = result[core]
    arrive([back])
    out_ref[:, pl.ds(pl.multiple_of((1 - core) * half, half), half)] = half_in[...]
    for copy in started:
        copy.wait_send()


GROUPS = 2
VMEM_MIB = 60


def widen(src, wide, first, rows):
    def step(i, carry):
        at = pl.ds(pl.multiple_of(first + i * 384, 384), 384)
        wide[at, :] = src[at, :].astype(jnp.float32)
        return carry

    lax.fori_loop(0, rows // 384, step, 0)


def narrow(wide, dst, first, rows):
    def step(i, carry):
        at = pl.ds(pl.multiple_of(first + i * 384, 384), 384)
        dst[at, :] = wide[at, :].astype(jnp.bfloat16)
        return carry

    lax.fori_loop(0, rows // 384, step, 0)


def peer_at(group, i, sign):
    s, p = lax.axis_index("seq"), lax.axis_index("exp")
    i = i + group * (lax.axis_size("seq") * lax.axis_size("exp") // GROUPS)
    turn, i = i // 32, lax.rem(i, 32)
    along_x, along_y, across = i // 8, lax.rem(i // 2, 4), lax.rem(i, 2)
    along_z = lax.rem(turn + 8 - along_x - along_y, 4)
    x = lax.rem(s // 2 + sign * along_x + 4, 4)
    y = lax.rem(p // 4 + sign * along_y + 4, 4)
    z = lax.rem(lax.rem(p, 4) + sign * along_z + 4, 4)
    return (2 * x + lax.rem(s + across, 2), 4 * y + z)


def place_of(expert):
    s, p = lax.axis_index("seq"), lax.axis_index("exp")
    to_s, to_p = expert >> 4, expert & 15
    along_x = ((to_s >> 1) - s // 2) & 3
    along_y = ((to_p >> 2) - p // 4) & 3
    along_z = (to_p - p) & 3
    across = (to_s + s) & 1
    turn = (along_x + along_y + along_z) & 3
    return turn * 32 + along_x * 8 + along_y * 2 + across


def exchange_start(group, sign, src, dst, send_sem, recv_sem, own_sem, chunk):
    members = src.shape[0] // chunk // GROUPS

    def step(i, carry):
        at = pl.ds(pl.multiple_of((group * members + i) * chunk, chunk), chunk)
        pltpu.make_async_remote_copy(
            src_ref=src.at[at],
            dst_ref=dst.at[at],
            send_sem=send_sem.at[group],
            recv_sem=recv_sem.at[group],
            device_id=peer_at(group, i, sign),
            device_id_type=MESH,
        ).start()
        return carry

    if group == 0:
        own = pl.ds(0, chunk)
        pltpu.make_async_copy(src.at[own], dst.at[own], own_sem).start()
    lax.fori_loop(1 if group == 0 else 0, members, step, 0)


def group_rows(group, src, chunk):
    members = src.shape[0] // chunk // GROUPS
    first = group * members + (1 if group == 0 else 0)
    return pl.ds(first * chunk, ((group + 1) * members - first) * chunk)


def exchange_wait(group, src, dst, recv_sem, own_sem, chunk):
    if group == 0:
        own = pl.ds(0, chunk)
        pltpu.make_async_copy(src.at[own], dst.at[own], own_sem).wait()
    at = group_rows(group, src, chunk)
    pltpu.make_async_copy(src.at[at], dst.at[at], recv_sem.at[group]).wait()


def exchange_sent(group, src, dst, send_sem, chunk):
    at = group_rows(group, src, chunk)
    pltpu.make_async_copy(src.at[at], dst.at[at], send_sem.at[group]).wait()


def experts_load(hbm, vmem, sem):
    copies = [pltpu.make_async_copy(a, b, sem.at[i]) for i, (a, b) in enumerate(zip(hbm, vmem))]
    for copy in copies:
        copy.start()
    return copies


def experts_part(
    loads, h_ref, recon_out, error_out, grad_out, out_sem,
    encw, decw, expert_row, slot_row, encb_ref, decb_ref, picks,
    wide, send, recv, back, ret, slot_rows, centered, latent, gated, residue,
    own_sem, send_sem, recv_sem, send_back_sem, recv_back_sem,
):
    tokens, width = h_ref.shape
    slots = slot_rows.shape[0]
    latents = latent.shape[1]
    lanes = width // TILE
    members = lax.axis_size("seq") * lax.axis_size("exp") // GROUPS
    chunk = slots // (members * GROUPS) * lanes
    part_slots = slots // GROUPS
    part_rows = part_slots * lanes
    enc_copy, dec_copy, *small = loads
    for copy in small:
        copy.wait()
    capacity = slots // (members * GROUPS)
    target = jnp.where(
        slot_row[...] >= 0, place_of(expert_row[...]) * capacity + slot_row[...], slots
    )

    for group in range(GROUPS):
        first = group * part_rows
        place = lax.broadcasted_iota(jnp.int32, (part_slots, tokens), 0) + group * part_slots
        pick = jnp.where(place == target, 1.0, 0.0)
        free = (1.0 - jnp.sum(pick, axis=1, keepdims=True)) * EMPTY
        pick = pick.astype(jnp.bfloat16)
        picks[group * part_slots : (group + 1) * part_slots, :] = pick
        for n in range(lanes // 2):
            rows = jnp.dot(
                pick,
                h_ref[:, 2 * n * TILE : 2 * (n + 1) * TILE],
                preferred_element_type=jnp.float32,
            )
            if n == 0:
                rows = rows + free
            wide[pl.ds(first + 2 * n, part_slots, stride=lanes), :] = rows[:, :TILE]
            wide[pl.ds(first + 2 * n + 1, part_slots, stride=lanes), :] = rows[:, TILE:]
        narrow(wide, send, first, part_rows)
        exchange_start(group, 1, send, recv, send_sem, recv_sem, own_sem.at[0], chunk)

    enc_copy.wait()
    dec_copy.wait()
    for group in range(GROUPS):
        first = group * part_rows
        mine = slice(group * part_slots, (group + 1) * part_slots)
        exchange_wait(group, send, recv, recv_sem, own_sem.at[0], chunk)
        widen(recv, wide, first, part_rows)
        live = wide[pl.ds(first, part_slots, stride=lanes), :][:, :1] < 0.5 * EMPTY
        for c in range(lanes):
            at = slice(c * TILE, (c + 1) * TILE)
            part = wide[pl.ds(first + c, part_slots, stride=lanes), :]
            if c < 2:
                part = jnp.where(live, part, 0.0)
            slot_rows[mine, at] = part.astype(jnp.bfloat16)
            centered[mine, at] = (part - decb_ref[:, at]).astype(jnp.bfloat16)
        for n in range(latents // 256):
            at = slice(n * 256, (n + 1) * 256)
            pre = jnp.dot(centered[mine, :], encw[:, at], preferred_element_type=jnp.float32)
            act = jnp.maximum(pre + encb_ref[:, at], 0.0)
            latent[mine, at] = act.astype(jnp.bfloat16)
            gated[mine, at] = jnp.where(live, act, 0.0).astype(jnp.bfloat16)
        for n in range(lanes // 2):
            at = slice(2 * n * TILE, 2 * (n + 1) * TILE)
            rebuilt = jnp.dot(latent[mine, :], decw[:, at], preferred_element_type=jnp.float32)
            rebuilt = (rebuilt + decb_ref[:, at]).astype(jnp.bfloat16).astype(jnp.float32)
            error = rebuilt - slot_rows[mine, at].astype(jnp.float32)
            residue[mine, at] = error.astype(jnp.bfloat16)
            wide[pl.ds(first + 2 * n, part_slots, stride=lanes), :] = rebuilt[:, :TILE]
            wide[pl.ds(first + 2 * n + 1, part_slots, stride=lanes), :] = rebuilt[:, TILE:]
        narrow(wide, back, first, part_rows)
        exchange_start(group, -1, back, ret, send_back_sem, recv_back_sem, own_sem.at[1], chunk)

    outs = []
    for n in range(latents // 256):
        at = slice(n * 256, (n + 1) * 256)
        decw[at, :] = lax.dot_general(
            gated[:, at], residue[...], (((0,), (0,)), ((), ())),
            preferred_element_type=jnp.float32,
        ).astype(jnp.bfloat16)
        rows = pl.ds(n * 256, 256)
        outs.append(pltpu.make_async_copy(decw.at[rows], grad_out.at[rows], out_sem.at[3 + n]))
        outs[-1].start()

    def gather_back(rows):
        return lax.dot_general(
            picks[...], rows, (((0,), (0,)), ((), ())), preferred_element_type=jnp.float32
        )

    kept = gather_back(jnp.ones((slots, TILE), jnp.bfloat16))[:, :1] > 0.5
    for group in range(GROUPS):
        first = group * part_rows
        mine = slice(group * part_slots, (group + 1) * part_slots)
        exchange_wait(group, back, ret, recv_back_sem, own_sem.at[1], chunk)
        widen(ret, wide, first, part_rows)
        for c in range(lanes):
            slot_rows[mine, c * TILE : (c + 1) * TILE] = wide[
                pl.ds(first + c, part_slots, stride=lanes), :
            ].astype(jnp.bfloat16)
    for n in range(width // 256):
        at = slice(n * 256, (n + 1) * 256)
        rows = jnp.where(kept, gather_back(slot_rows[:, at]), decb_ref[:, at]).astype(jnp.bfloat16)
        centered[:tokens, at] = rows
        error = rows.astype(jnp.float32) - h_ref[:, at].astype(jnp.float32)
        centered[tokens : 2 * tokens, at] = error.astype(jnp.bfloat16)
    for i, out in enumerate((recon_out, error_out)):
        rows = centered.at[pl.ds(i * tokens, tokens)]
        outs.append(pltpu.make_async_copy(rows, out, out_sem.at[1 + i]))
        outs[-1].start()
    for copy in outs:
        copy.wait()
    for group in range(GROUPS):
        exchange_sent(group, send, recv, send_sem, chunk)
        exchange_sent(group, back, ret, send_back_sem, chunk)


def whole_kernel(
    q_hbm, k_hbm, v_hbm, doc_hbm, w_hbm,
    expert_hbm, slot_hbm, encw_hbm, encb_hbm, decw_hbm, decb_hbm,
    h_out, recon_out, error_out, grad_out, *scratch,
):
    first, second = scratch[:13], scratch[13:-3]
    load_sem, out_sem, h_ref = scratch[-3:]
    loads = experts_load(
        (encw_hbm, decw_hbm, expert_hbm, slot_hbm, encb_hbm, decb_hbm), second[:6], load_sem
    )
    attention_part(q_hbm, k_hbm, v_hbm, doc_hbm, w_hbm, h_ref, *first)
    h_copy = pltpu.make_async_copy(h_ref, h_out, out_sem.at[0])
    h_copy.start()
    experts_part(loads, h_ref, recon_out, error_out, grad_out, out_sem, *second)
    h_copy.wait()


def run_whole(
    query, key, value, doc_all, out_weight, experts, slot_ids, enc_weight, enc_bias, dec_weight,
    dec_bias, seq_groups, slots,
):
    tokens, q_width = query.shape
    kv_width = key.shape[1]
    span = tokens * seq_groups
    rows, width = out_weight.shape
    latents = enc_bias.shape[1]
    lanes = width // TILE
    hbm = pl.BlockSpec(memory_space=pl.ANY)
    dma = pltpu.SemaphoreType.DMA
    copies = 128

    def half(*shape):
        return pltpu.VMEM(shape, jnp.bfloat16)

    def full(*shape):
        return pltpu.VMEM(shape, jnp.float32)

    return pl.pallas_call(
        whole_kernel,
        out_shape=(
            *[jax.ShapeDtypeStruct((tokens, width), jnp.bfloat16)] * 3,
            jax.ShapeDtypeStruct((latents, width), jnp.bfloat16),
        ),
        in_specs=[hbm] * 11,
        out_specs=(hbm,) * 4,
        scratch_shapes=[
            pltpu.VMEM((1, span), jnp.int32),
            half(tokens, q_width),
            half(seq_groups, tokens, 2 * kv_width),
            *[half(4, 2, 4, 4, rows, wide) for _, wide in PARTS],
            half(2, tokens, q_width),
            full(tokens, span),
            half(2, tokens, width // 2),
            half(tokens, width // 2),
            dma((copies,)),
            dma((copies,)),
            dma((7,)),
            half(width, latents),
            half(latents, width),
            pltpu.VMEM((1, tokens), jnp.int32),
            pltpu.VMEM((1, tokens), jnp.int32),
            full(1, latents),
            full(1, width),
            half(slots, tokens),
            full(slots * lanes, TILE),
            *[half(slots * lanes, TILE)] * 4,
            half(slots, width),
            half(slots, width),
            half(slots, latents),
            half(slots, latents),
            half(slots, width),
            dma((2,)),
            *[dma((GROUPS,))] * 4,
            dma((6,)),
            dma((3 + latents // 256,)),
            half(tokens, width),
        ],
        compiler_params=pltpu.CompilerParams(
            collective_id=0, has_side_effects=True, vmem_limit_bytes=VMEM_MIB * 2**20
        ),
    )(
        query, key, value, doc_all, out_weight, experts, slot_ids, enc_weight, enc_bias,
        dec_weight, dec_bias[None, :],
    )


def finish_kernel(*refs):
    sources, targets, held, sems = refs[:4], refs[4:8], refs[8:12], refs[12:]
    pairs = []
    for source, hold, target in zip(sources, held, targets):
        rows = source.shape[0]
        for first in range(0, rows, 192):
            at = pl.ds(first, min(192, rows - first))
            i = len(pairs)
            pairs.append(
                (
                    pltpu.make_async_copy(source.at[at], hold.at[at], sems[0].at[i]),
                    pltpu.make_async_copy(hold.at[at], target.at[at], sems[1].at[i]),
                )
            )
            pairs[-1][0].start()
    for fetch, store in pairs:
        fetch.wait()
        store.start()
    for fetch, store in pairs:
        store.wait()


def run_finish(*arrays):
    hbm = pl.BlockSpec(memory_space=pl.ANY)
    return pl.pallas_call(
        finish_kernel,
        out_shape=tuple(jax.ShapeDtypeStruct(a.shape, a.dtype) for a in arrays),
        in_specs=[hbm] * 4,
        out_specs=(hbm,) * 4,
        scratch_shapes=[
            *[pltpu.VMEM(a.shape, a.dtype) for a in arrays],
            pltpu.SemaphoreType.DMA((16,)),
            pltpu.SemaphoreType.DMA((16,)),
        ],
        compiler_params=pltpu.CompilerParams(vmem_limit_bytes=VMEM_MIB * 2**20),
    )(*arrays)


def shards(
    query_rows,
    key_rows,
    value_matrix,
    doc_ids,
    out_weight,
    enc_weight,
    enc_bias,
    dec_weight,
    dec_bias,
    expert_ids,
    slot_ids,
):
    local_tokens = query_rows.shape[1]
    seq_groups = lax.axis_size("seq")
    experts_all = enc_weight.shape[0] * seq_groups * lax.axis_size("exp")
    slot_count = 2 * local_tokens // experts_all * experts_all
    outputs = run_whole(
        query_rows[0], key_rows[0], value_matrix[0], doc_ids, out_weight, expert_ids, slot_ids,
        enc_weight[0], enc_bias, dec_weight[0], dec_bias, seq_groups, slot_count,
    )
    harvested, reconstruction, error_rows, dec_grad = run_finish(*outputs)
    return (harvested[None], reconstruction[None], error_rows[None], dec_grad[None])


def solution(mesh):
    return jax.shard_map(
        shards,
        mesh=mesh,
        in_specs=(
            P("exp", "seq", None),
            P("exp", "seq", None),
            P("exp", "seq", None),
            P("exp", None),
            P(("seq", "exp"), None),
            P(("seq", "exp"), None, None),
            P(("seq", "exp"), None),
            P(("seq", "exp"), None, None),
            P(),
            P("exp", "seq"),
            P("exp", "seq"),
        ),
        out_specs=(
            P("exp", "seq", None),
            P("exp", "seq", None),
            P("exp", "seq", None),
            P(("seq", "exp"), None, None),
        ),
        check_vma=False,
    )
```

```python
import math

import jax
import jax.numpy as jnp
from jax import lax
from jax.experimental import pallas as pl
from jax.experimental.pallas import tpu as pltpu
from jax.sharding import PartitionSpec as P

HEAD_DIMENSION = 128
MESH = pl.DeviceIdType.MESH
TILE = 128
EMPTY = 1e30
PARTS = ((0, 384), (384, 256), (640, 384))
ORDERS = ("xyz", "yzx", "xzy")


def attention_part(
    q_hbm, k_hbm, v_hbm, doc_hbm, w_hbm,
    out_ref,
    doc_row, queries, kv, w_a, w_b, w_c, attended, bias, result, half_in,
    send_sem, recv_sem, local_sem,
):
    s, p = lax.axis_index("seq"), lax.axis_index("exp")
    place = {"x": s // 2, "y": p // 4, "z": lax.rem(p, 4)}
    core = lax.rem(s, 2)
    tokens = queries.shape[0]
    kv_width = k_hbm.shape[1]
    span = kv.shape[0] * tokens
    half = out_ref.shape[1] // 2
    heads = queries.shape[1] // HEAD_DIMENSION
    group = heads // (kv_width // HEAD_DIMENSION)
    scale = math.log2(math.e) / math.sqrt(HEAD_DIMENSION)
    parts = (w_a, w_b, w_c)
    partner = (2 * place["x"] + 1 - core, p)

    def beside(axis, step):
        at = dict(place)
        at[axis] = lax.rem(at[axis] + step + 4, 4)
        return (2 * at["x"] + core, 4 * at["y"] + at["z"])

    peers = [partner] + [beside(axis, step) for axis in "xyz" for step in (1, -1)]
    barrier = pltpu.get_barrier_semaphore()
    for peer in peers:
        pl.semaphore_signal(barrier, inc=1, device_id=peer, device_id_type=MESH)

    started = []

    def send(src, dst, peer, go=True):
        copy = pltpu.make_async_remote_copy(
            src_ref=src,
            dst_ref=dst,
            send_sem=send_sem.at[len(started)],
            recv_sem=recv_sem.at[len(started)],
            device_id=peer,
            device_id_type=MESH,
        )
        started.append(copy)
        if go:
            copy.start()
        return copy

    def arrive(copies):
        for copy in copies:
            copy.wait_recv()

    own = [
        (k_hbm, kv.at[s, :, pl.ds(0, kv_width)]),
        (v_hbm, kv.at[s, :, pl.ds(kv_width, kv_width)]),
    ]
    for (first, wide), buffer in zip(PARTS, parts):
        columns = pl.ds(pl.multiple_of(core * half + first, TILE), wide)
        own.append((w_hbm.at[:, columns], buffer.at[place["x"], core, place["y"], place["z"]]))
    own.append((doc_hbm, doc_row))
    own.append((q_hbm, queries))
    own = [pltpu.make_async_copy(a, b, local_sem.at[i]) for i, (a, b) in enumerate(own)]
    for copy in own:
        copy.start()
    own[0].wait()
    own[1].wait()
    pl.semaphore_wait(barrier, len(peers))

    w_pair = []
    for (first, wide), buffer in zip(PARTS, parts):
        columns = pl.ds(pl.multiple_of((1 - core) * half + first, TILE), wide)
        w_pair.append(
            send(
                w_hbm.at[:, columns],
                buffer.at[place["x"], core, place["y"], place["z"]],
                partner,
            )
        )

    def view(part, offsets, row=None):
        at = {}
        for axis, offset in zip(ORDERS[part], offsets):
            if offset is None:
                at[axis] = pl.ds(0, 4)
            else:
                at[axis] = pl.ds(lax.rem(place[axis] + offset + 4, 4), 1)
        rows = pl.ds(0, 2) if row is None else pl.ds(row, 1)
        return parts[part].at[at["x"], rows, at["y"], at["z"]]

    def near(stage, offsets):
        copies = []
        for part in range(3):
            block = view(part, offsets)
            for step in (1, -1):
                copies.append(send(block, block, beside(ORDERS[part][stage], step)))
        return copies

    def far(stage, offsets, go=True):
        copies = []
        for part in range(3):
            for step, row in ((1, 0), (-1, 1)):
                at = offsets[:stage] + (-step,) + offsets[stage + 1 :]
                block = view(part, at, row)
                copies.append(send(block, block, beside(ORDERS[part][stage], step), go))
        return copies

    def attend(quarter, blocks):
        keys = blocks * tokens

        def one_head(h, carry):
            g = h // group
            q_at = pl.ds(pl.multiple_of(h * HEAD_DIMENSION, HEAD_DIMENSION), HEAD_DIMENSION)
            k_at = pl.ds(pl.multiple_of(g * HEAD_DIMENSION, HEAD_DIMENSION), HEAD_DIMENSION)
            v_at = pl.ds(
                pl.multiple_of(kv_width + g * HEAD_DIMENSION, HEAD_DIMENSION), HEAD_DIMENSION
            )
            key_part = kv[:blocks, :, k_at].reshape(keys, HEAD_DIMENSION)
            value_part = kv[:blocks, :, v_at].reshape(keys, HEAD_DIMENSION)
            scores = lax.dot_general(
                queries[:, q_at], key_part, (((1,), (1,)), ((), ())),
                preferred_element_type=jnp.float32,
            )
            scores = scores + bias[:, :keys]
            highest = jnp.max(scores, axis=1, keepdims=True)
            weights = jnp.exp2((scores - highest) * scale)
            total = jnp.sum(weights, axis=1, keepdims=True)
            mixed = jnp.dot(
                weights.astype(jnp.bfloat16), value_part, preferred_element_type=jnp.float32
            )
            attended[core, :, q_at] = (mixed / total).astype(jnp.bfloat16)
            return carry

        def four(i, carry):
            for j in range(4):
                one_head(4 * i + j + quarter * (heads // 4), carry)
            return carry

        lax.fori_loop(0, heads // 16, four, 0)

    def attend_some(quarter):
        for chips in range(1, 5):

            @pl.when(place["x"] == chips - 1)
            def _():
                attend(quarter, 2 * chips)

    def across(quarter):
        wide = heads // 4 * HEAD_DIMENSION
        piece = attended.at[core, :, pl.ds(pl.multiple_of(quarter * wide, wide), wide)]
        return pltpu.make_async_remote_copy(
            src_ref=piece,
            dst_ref=piece,
            send_sem=send_sem.at[124 + quarter],
            recv_sem=recv_sem.at[124 + quarter],
            device_id=partner,
            device_id_type=MESH,
        )

    arrive(w_pair)
    for copy in own[2:5]:
        copy.wait()
    near_1 = near(0, (0, 0, 0))
    kv_near = [send(kv.at[s], kv.at[s], beside("x", step)) for step in (1, -1)]
    kv_own_pair = send(kv.at[s], kv.at[s], partner)
    near_2 = near(1, (0, 0, 0))
    near_3 = near(2, (0, 0, 0))
    own[5].wait()
    rows_at = s * tokens + lax.broadcasted_iota(jnp.int32, (tokens, span), 0)
    keys_at = lax.broadcasted_iota(jnp.int32, (tokens, span), 1)
    doc_all = doc_row[...].astype(jnp.float32)
    doc_mine = jnp.sum(jnp.where(rows_at == keys_at, doc_all, 0.0), axis=1, keepdims=True)
    visible = (rows_at >= keys_at) & (doc_mine == doc_all)
    bias[...] = jnp.where(visible, 0.0, -EMPTY)
    own[6].wait()
    arrive([kv_own_pair])
    arrive(near_1)
    far_1 = far(0, (None, 0, 0))
    for offset in (-1, 1):
        near_2 += near(1, (offset, 0, 0))
        near_3 += near(2, (offset, 0, 0))
    arrive(far_1)
    near_2 += near(1, (2, 0, 0))
    near_3 += near(2, (2, 0, 0))
    arrive(kv_near)
    kv_far = []
    for step, first in ((1, 0), (-1, tokens // 2)):
        origin = 2 * lax.rem(place["x"] - step + 4, 4) + core
        piece = kv.at[origin, pl.ds(first, tokens // 2)]
        kv_far.append(send(piece, piece, beside("x", step)))
    kv_pair = []
    for step in (1, -1):
        piece = kv.at[2 * lax.rem(place["x"] - step + 4, 4) + core]
        kv_pair.append(send(piece, piece, partner))
    arrive(near_2)
    far_2 = far(1, (None, None, 0))
    near_3b = near(2, (None, -1, 0)) + near(2, (None, 1, 0))
    arrive(kv_far)
    piece = kv.at[2 * lax.rem(place["x"] + 2, 4) + core]
    kv_pair.append(send(piece, piece, partner))
    arrive(far_2)
    near_3c = near(2, (None, 2, 0))
    arrive(kv_pair)
    waves = (
        (near_3, far(2, (None, 0, None), False)),
        (near_3b, far(2, (None, -1, None), False) + far(2, (None, 1, None), False)),
        (near_3c, far(2, (None, 2, None), False)),
    )

    def quarter_step(quarter, carry):
        attend_some(quarter)
        across(quarter).start()
        for i, (come, go) in enumerate(waves):

            @pl.when(quarter == i)
            def _():
                arrive(come)
                for copy in go:
                    copy.start()

        return carry

    lax.fori_loop(0, 4, quarter_step, 0)
    for quarter in range(4):
        across(quarter).wait()
    far_3 = waves[0][1] + waves[1][1] + waves[2][1]
    arrive(far_3)

    rows = attended.shape[1] * 2
    for (first, wide), buffer in zip(PARTS, parts):
        both = jnp.dot(
            attended[...].reshape(rows, heads * HEAD_DIMENSION),
            buffer[...].reshape(heads * HEAD_DIMENSION, wide),
            preferred_element_type=jnp.float32,
        )
        result[:, :, first : first + wide] = both.astype(jnp.bfloat16).reshape(2, tokens, wide)
    back = send(result.at[1 - core], half_in, partner)
    out_ref[:, pl.ds(pl.multiple_of(core * half, half), half)] = result[core]
    arrive([back])
    out_ref[:, pl.ds(pl.multiple_of((1 - core) * half, half), half)] = half_in[...]
    for copy in started:
        copy.wait_send()


GROUPS = 2
VMEM_MIB = 60


def widen(src, wide, first, rows):
    def step(i, carry):
        at = pl.ds(pl.multiple_of(first + i * 384, 384), 384)
        wide[at, :] = src[at, :].astype(jnp.float32)
        return carry

    lax.fori_loop(0, rows // 384, step, 0)


def narrow(wide, dst, first, rows):
    def step(i, carry):
        at = pl.ds(pl.multiple_of(first + i * 384, 384), 384)
        dst[at, :] = wide[at, :].astype(jnp.bfloat16)
        return carry

    lax.fori_loop(0, rows // 384, step, 0)


def peer_at(group, i, sign):
    s, p = lax.axis_index("seq"), lax.axis_index("exp")
    i = i + group * (lax.axis_size("seq") * lax.axis_size("exp") // GROUPS)
    turn, i = i // 32, lax.rem(i, 32)
    along_x, along_y, across = i // 8, lax.rem(i // 2, 4), lax.rem(i, 2)
    along_z = lax.rem(turn + 8 - along_x - along_y, 4)
    x = lax.rem(s // 2 + sign * along_x + 4, 4)
    y = lax.rem(p // 4 + sign * along_y + 4, 4)
    z = lax.rem(lax.rem(p, 4) + sign * along_z + 4, 4)
    return (2 * x + lax.rem(s + across, 2), 4 * y + z)


def place_of(expert):
    s, p = lax.axis_index("seq"), lax.axis_index("exp")
    to_s, to_p = expert >> 4, expert & 15
    along_x = ((to_s >> 1) - s // 2) & 3
    along_y = ((to_p >> 2) - p // 4) & 3
    along_z = (to_p - p) & 3
    across = (to_s + s) & 1
    turn = (along_x + along_y + along_z) & 3
    return turn * 32 + along_x * 8 + along_y * 2 + across


def exchange_start(group, sign, src, dst, send_sem, recv_sem, own_sem, chunk):
    members = src.shape[0] // chunk // GROUPS

    def step(i, carry):
        at = pl.ds(pl.multiple_of((group * members + i) * chunk, chunk), chunk)
        pltpu.make_async_remote_copy(
            src_ref=src.at[at],
            dst_ref=dst.at[at],
            send_sem=send_sem.at[group],
            recv_sem=recv_sem.at[group],
            device_id=peer_at(group, i, sign),
            device_id_type=MESH,
        ).start()
        return carry

    if group == 0:
        own = pl.ds(0, chunk)
        pltpu.make_async_copy(src.at[own], dst.at[own], own_sem).start()
    lax.fori_loop(1 if group == 0 else 0, members, step, 0)


def group_rows(group, src, chunk):
    members = src.shape[0] // chunk // GROUPS
    first = group * members + (1 if group == 0 else 0)
    return pl.ds(first * chunk, ((group + 1) * members - first) * chunk)


def exchange_wait(group, src, dst, recv_sem, own_sem, chunk):
    if group == 0:
        own = pl.ds(0, chunk)
        pltpu.make_async_copy(src.at[own], dst.at[own], own_sem).wait()
    at = group_rows(group, src, chunk)
    pltpu.make_async_copy(src.at[at], dst.at[at], recv_sem.at[group]).wait()


def exchange_sent(group, src, dst, send_sem, chunk):
    at = group_rows(group, src, chunk)
    pltpu.make_async_copy(src.at[at], dst.at[at], send_sem.at[group]).wait()


def experts_load(hbm, vmem, sem):
    copies = [pltpu.make_async_copy(a, b, sem.at[i]) for i, (a, b) in enumerate(zip(hbm, vmem))]
    for copy in copies:
        copy.start()
    return copies


def experts_part(
    loads, h_ref, recon_out, error_out, grad_out, out_sem,
    encw, decw, expert_row, slot_row, encb_ref, decb_ref, picks,
    wide, send, recv, back, ret, slot_rows, centered, latent, gated, residue,
    own_sem, send_sem, recv_sem, send_back_sem, recv_back_sem,
):
    tokens, width = h_ref.shape
    slots = slot_rows.shape[0]
    latents = latent.shape[1]
    lanes = width // TILE
    members = lax.axis_size("seq") * lax.axis_size("exp") // GROUPS
    chunk = slots // (members * GROUPS) * lanes
    part_slots = slots // GROUPS
    part_rows = part_slots * lanes
    enc_copy, dec_copy, *small = loads
    for copy in small:
        copy.wait()
    capacity = slots // (members * GROUPS)
    target = jnp.where(
        slot_row[...] >= 0, place_of(expert_row[...]) * capacity + slot_row[...], slots
    )

    for group in range(GROUPS):
        first = group * part_rows
        place = lax.broadcasted_iota(jnp.int32, (part_slots, tokens), 0) + group * part_slots
        pick = jnp.where(place == target, 1.0, 0.0)
        free = (1.0 - jnp.sum(pick, axis=1, keepdims=True)) * EMPTY
        pick = pick.astype(jnp.bfloat16)
        picks[group * part_slots : (group + 1) * part_slots, :] = pick
        for n in range(lanes // 2):
            rows = jnp.dot(
                pick,
                h_ref[:, 2 * n * TILE : 2 * (n + 1) * TILE],
                preferred_element_type=jnp.float32,
            )
            if n == 0:
                rows = rows + free
            wide[pl.ds(first + 2 * n, part_slots, stride=lanes), :] = rows[:, :TILE]
            wide[pl.ds(first + 2 * n + 1, part_slots, stride=lanes), :] = rows[:, TILE:]
        narrow(wide, send, first, part_rows)
        exchange_start(group, 1, send, recv, send_sem, recv_sem, own_sem.at[0], chunk)

    enc_copy.wait()
    dec_copy.wait()
    for group in range(GROUPS):
        first = group * part_rows
        mine = slice(group * part_slots, (group + 1) * part_slots)
        exchange_wait(group, send, recv, recv_sem, own_sem.at[0], chunk)
        widen(recv, wide, first, part_rows)
        live = wide[pl.ds(first, part_slots, stride=lanes), :][:, :1] < 0.5 * EMPTY
        for c in range(lanes):
            at = slice(c * TILE, (c + 1) * TILE)
            part = wide[pl.ds(first + c, part_slots, stride=lanes), :]
            if c < 2:
                part = jnp.where(live, part, 0.0)
            slot_rows[mine, at] = part.astype(jnp.bfloat16)
            centered[mine, at] = (part - decb_ref[:, at]).astype(jnp.bfloat16)
        for n in range(latents // 256):
            at = slice(n * 256, (n + 1) * 256)
            pre = jnp.dot(centered[mine, :], encw[:, at], preferred_element_type=jnp.float32)
            act = jnp.maximum(pre + encb_ref[:, at], 0.0)
            latent[mine, at] = act.astype(jnp.bfloat16)
            gated[mine, at] = jnp.where(live, act, 0.0).astype(jnp.bfloat16)
        for n in range(lanes // 2):
            at = slice(2 * n * TILE, 2 * (n + 1) * TILE)
            rebuilt = jnp.dot(latent[mine, :], decw[:, at], preferred_element_type=jnp.float32)
            rebuilt = (rebuilt + decb_ref[:, at]).astype(jnp.bfloat16).astype(jnp.float32)
            error = rebuilt - slot_rows[mine, at].astype(jnp.float32)
            residue[mine, at] = error.astype(jnp.bfloat16)
            wide[pl.ds(first + 2 * n, part_slots, stride=lanes), :] = rebuilt[:, :TILE]
            wide[pl.ds(first + 2 * n + 1, part_slots, stride=lanes), :] = rebuilt[:, TILE:]
        narrow(wide, back, first, part_rows)
        exchange_start(group, -1, back, ret, send_back_sem, recv_back_sem, own_sem.at[1], chunk)

    outs = []
    for n in range(latents // 256):
        at = slice(n * 256, (n + 1) * 256)
        decw[at, :] = lax.dot_general(
            gated[:, at], residue[...], (((0,), (0,)), ((), ())),
            preferred_element_type=jnp.float32,
        ).astype(jnp.bfloat16)
        rows = pl.ds(n * 256, 256)
        outs.append(pltpu.make_async_copy(decw.at[rows], grad_out.at[rows], out_sem.at[3 + n]))
        outs[-1].start()

    def gather_back(rows):
        return lax.dot_general(
            picks[...], rows, (((0,), (0,)), ((), ())), preferred_element_type=jnp.float32
        )

    kept = gather_back(jnp.ones((slots, TILE), jnp.bfloat16))[:, :1] > 0.5
    for group in range(GROUPS):
        first = group * part_rows
        mine = slice(group * part_slots, (group + 1) * part_slots)
        exchange_wait(group, back, ret, recv_back_sem, own_sem.at[1], chunk)
        widen(ret, wide, first, part_rows)
        for c in range(lanes):
            slot_rows[mine, c * TILE : (c + 1) * TILE] = wide[
                pl.ds(first + c, part_slots, stride=lanes), :
            ].astype(jnp.bfloat16)
    for n in range(width // 256):
        at = slice(n * 256, (n + 1) * 256)
        rows = jnp.where(kept, gather_back(slot_rows[:, at]), decb_ref[:, at]).astype(jnp.bfloat16)
        centered[:tokens, at] = rows
        error = rows.astype(jnp.float32) - h_ref[:, at].astype(jnp.float32)
        centered[tokens : 2 * tokens, at] = error.astype(jnp.bfloat16)
    for i, out in enumerate((recon_out, error_out)):
        rows = centered.at[pl.ds(i * tokens, tokens)]
        outs.append(pltpu.make_async_copy(rows, out, out_sem.at[1 + i]))
        outs[-1].start()
    for copy in outs:
        copy.wait()
    for group in range(GROUPS):
        exchange_sent(group, send, recv, send_sem, chunk)
        exchange_sent(group, back, ret, send_back_sem, chunk)


def whole_kernel(
    q_hbm, k_hbm, v_hbm, doc_hbm, w_hbm,
    expert_hbm, slot_hbm, encw_hbm, encb_hbm, decw_hbm, decb_hbm,
    h_out, recon_out, error_out, grad_out, *scratch,
):
    first, second = scratch[:13], scratch[13:-3]
    load_sem, out_sem, h_ref = scratch[-3:]
    loads = experts_load(
        (encw_hbm, decw_hbm, expert_hbm, slot_hbm, encb_hbm, decb_hbm), second[:6], load_sem
    )
    attention_part(q_hbm, k_hbm, v_hbm, doc_hbm, w_hbm, h_ref, *first)
    h_copy = pltpu.make_async_copy(h_ref, h_out, out_sem.at[0])
    h_copy.start()
    experts_part(loads, h_ref, recon_out, error_out, grad_out, out_sem, *second)
    h_copy.wait()


def run_whole(
    query, key, value, doc_all, out_weight, experts, slot_ids, enc_weight, enc_bias, dec_weight,
    dec_bias, seq_groups, slots,
):
    tokens, q_width = query.shape
    kv_width = key.shape[1]
    span = tokens * seq_groups
    rows, width = out_weight.shape
    latents = enc_bias.shape[1]
    lanes = width // TILE
    hbm = pl.BlockSpec(memory_space=pl.ANY)
    dma = pltpu.SemaphoreType.DMA
    copies = 128

    def half(*shape):
        return pltpu.VMEM(shape, jnp.bfloat16)

    def full(*shape):
        return pltpu.VMEM(shape, jnp.float32)

    return pl.pallas_call(
        whole_kernel,
        out_shape=(
            *[jax.ShapeDtypeStruct((tokens, width), jnp.bfloat16)] * 3,
            jax.ShapeDtypeStruct((latents, width), jnp.bfloat16),
        ),
        in_specs=[hbm] * 11,
        out_specs=(hbm,) * 4,
        scratch_shapes=[
            pltpu.VMEM((1, span), jnp.int32),
            half(tokens, q_width),
            half(seq_groups, tokens, 2 * kv_width),
            *[half(4, 2, 4, 4, rows, wide) for _, wide in PARTS],
            half(2, tokens, q_width),
            full(tokens, span),
            half(2, tokens, width // 2),
            half(tokens, width // 2),
            dma((copies,)),
            dma((copies,)),
            dma((7,)),
            half(width, latents),
            half(latents, width),
            pltpu.VMEM((1, tokens), jnp.int32),
            pltpu.VMEM((1, tokens), jnp.int32),
            full(1, latents),
            full(1, width),
            half(slots, tokens),
            full(slots * lanes, TILE),
            *[half(slots * lanes, TILE)] * 4,
            half(slots, width),
            half(slots, width),
            half(slots, latents),
            half(slots, latents),
            half(slots, width),
            dma((2,)),
            *[dma((GROUPS,))] * 4,
            dma((6,)),
            dma((3 + latents // 256,)),
            half(tokens, width),
        ],
        compiler_params=pltpu.CompilerParams(
            collective_id=0, has_side_effects=True, vmem_limit_bytes=VMEM_MIB * 2**20
        ),
    )(
        query, key, value, doc_all, out_weight, experts, slot_ids, enc_weight, enc_bias,
        dec_weight, dec_bias[None, :],
    )


def finish_kernel(*refs):
    sources, targets, held, sems = refs[:4], refs[4:8], refs[8:12], refs[12:]
    pairs = []
    for source, hold, target in zip(sources, held, targets):
        rows = source.shape[0]
        for first in range(0, rows, 192):
            at = pl.ds(first, min(192, rows - first))
            i = len(pairs)
            pairs.append(
                (
                    pltpu.make_async_copy(source.at[at], hold.at[at], sems[0].at[i]),
                    pltpu.make_async_copy(hold.at[at], target.at[at], sems[1].at[i]),
                )
            )
            pairs[-1][0].start()
    for fetch, store in pairs:
        fetch.wait()
        store.start()
    for fetch, store in pairs:
        store.wait()


def run_finish(*arrays):
    hbm = pl.BlockSpec(memory_space=pl.ANY)
    return pl.pallas_call(
        finish_kernel,
        out_shape=tuple(jax.ShapeDtypeStruct(a.shape, a.dtype) for a in arrays),
        in_specs=[hbm] * 4,
        out_specs=(hbm,) * 4,
        scratch_shapes=[
            *[pltpu.VMEM(a.shape, a.dtype) for a in arrays],
            pltpu.SemaphoreType.DMA((16,)),
            pltpu.SemaphoreType.DMA((16,)),
        ],
        compiler_params=pltpu.CompilerParams(vmem_limit_bytes=VMEM_MIB * 2**20),
    )(*arrays)


def shards(
    query_rows,
    key_rows,
    value_matrix,
    doc_ids,
    out_weight,
    enc_weight,
    enc_bias,
    dec_weight,
    dec_bias,
    expert_ids,
    slot_ids,
):
    local_tokens = query_rows.shape[1]
    seq_groups = lax.axis_size("seq")
    experts_all = enc_weight.shape[0] * seq_groups * lax.axis_size("exp")
    slot_count = 2 * local_tokens // experts_all * experts_all
    outputs = run_whole(
        query_rows[0], key_rows[0], value_matrix[0], doc_ids, out_weight, expert_ids, slot_ids,
        enc_weight[0], enc_bias, dec_weight[0], dec_bias, seq_groups, slot_count,
    )
    harvested, reconstruction, error_rows, dec_grad = run_finish(*outputs)
    return (harvested[None], reconstruction[None], error_rows[None], dec_grad[None])


def solution(mesh):
    return jax.shard_map(
        shards,
        mesh=mesh,
        in_specs=(
            P("exp", "seq", None),
            P("exp", "seq", None),
            P("exp", "seq", None),
            P("exp", None),
            P(("seq", "exp"), None),
            P(("seq", "exp"), None, None),
            P(("seq", "exp"), None),
            P(("seq", "exp"), None, None),
            P(),
            P("exp", "seq"),
            P("exp", "seq"),
        ),
        out_specs=(
            P("exp", "seq", None),
            P("exp", "seq", None),
            P("exp", "seq", None),
            P(("seq", "exp"), None, None),
        ),
        check_vma=False,
    )
```
